256 devices in a mesh: ia: 8 (over z_lo, core), wa: 4 (over y), ao: 8 (over z_hi, x).
Axes of the slice: x: 4, y: 4, z: 8 (z_hi: 2, z_lo: 4; z = z_hi * 4 + z_lo), core: 2. Of those that a mesh axis runs over, the one named last changes fastest.
Arguments:
- inputs: bfloat16 [1280, 12288], P('wa', ('ia', 'ao')), may hold values from -6 to 6
- out_grad: bfloat16 [1280, 12288], P('wa', ('ia', 'ao')), may hold values from -6 to 6
- preact: bfloat16 [1280, 24576], P('wa', 'ao'), may hold values from -6 to 6
- up_weight: bfloat16 [12288, 24576], P('ia', ('ao', 'wa')), may hold values from -0.0546875 to 0.0546875
- down_weight: bfloat16 [24576, 12288], P(('ao', 'wa'), 'ia'), may hold values from -0.0390625 to 0.0390625
Outputs:
- input_grad: bfloat16 [1280, 12288], P('wa', ('ia', 'ao'))
- up_grad: bfloat16 [12288, 24576], P('ia', ('ao', 'wa'))
- down_grad: bfloat16 [24576, 12288], P(('ao', 'wa'), 'ia')
The draws below stay inside these ranges and needn't reach their ends.
All inputs are finite; a program needn't handle non-finite values.
Results may differ from the reference program's by a relative error of at most 0.025.
Values may be sent and summed in bfloat16 or wider, within the bound.
A program may use at most 128 MiB of HBM per device.

```python
import jax
import jax.numpy as jnp
from jax import lax

D = 12288
FF = 24576
TOK_DEV = 320
TOKENS = 1280
N_IA = 8
N_WA = 4


def shard_levels(own_key, extent, cuts, low, largest):
    gain, own = 1.0, jax.random.fold_in(own_key, 6)
    for dim, shards_of in cuts:
        heights = jnp.exp(jax.random.uniform(jax.random.fold_in(own, dim), (shards_of,), jnp.float32, low / len(cuts), largest / len(cuts)))
        gain = gain * jnp.repeat(heights, extent[dim] // shards_of).reshape([-1 if axis == dim else 1 for axis in range(len(extent))])
    return gain


def centred(stream_key, dims, width, limit, split=(), dtype=jnp.bfloat16):
    array = jax.random.normal(stream_key, dims, jnp.float32) * width
    if len(split) > 0:
        array = shard_levels(stream_key, dims, split, -0.22, 0.18) * array
    return jnp.clip(array, min=-limit, max=limit).astype(dtype)


def setup_inputs(seed: int = 0) -> dict:
    seeds = jax.random.split(jax.random.key(seed), 6)
    return {
        "inputs": centred(seeds[0], (TOKENS, D), 1.0, 6.0, ((0, 4), (1, 64))),
        "out_grad": centred(seeds[1], (TOKENS, D), 1.0, 6.0, ((0, 4), (1, 64))),
        "preact": centred(seeds[2], (TOKENS, FF), 1.0, 6.0, ((0, 4), (1, 8))),
        "up_weight": centred(seeds[3], (D, FF), D ** -0.5, 0.0546875, ((0, 8), (1, 32))),
        "down_weight": centred(seeds[4], (FF, D), FF ** -0.5, 0.0390625, ((0, 32), (1, 8))),
    }


def gelu_parts(values):
    floats = values.astype(jnp.float32)
    square = floats * floats
    inner = 0.7978845608 * (floats + 0.044715 * floats * square)
    tangent = jnp.tanh(inner)
    activated = 0.5 * floats * (1.0 + tangent)
    derivative = 0.5 * (1.0 + tangent) + 0.5 * floats * (1.0 - tangent * tangent) * 0.7978845608 * (1.0 + 0.134145 * square)
    return activated, derivative


def rounded(values):
    return lax.optimization_barrier(values.astype(jnp.bfloat16)).astype(jnp.float32)


def reference(inputs, out_grad, preact, up_weight, down_weight):
    activated, derivative = gelu_parts(preact)
    activated = activated.astype(jnp.bfloat16)
    feat_width = D // N_IA
    act_grad = jnp.zeros((TOKENS, FF), jnp.float32)
    for member in range(N_IA):
        grad_cols = out_grad[:, member * feat_width:(member + 1) * feat_width]
        weight_cols = down_weight[:, member * feat_width:(member + 1) * feat_width]
        act_grad = act_grad + rounded(jnp.dot(grad_cols, weight_cols.T, preferred_element_type=jnp.float32))
    hidden_grad = (act_grad * derivative).astype(jnp.bfloat16)
    input_grad = jnp.dot(hidden_grad, up_weight.T, preferred_element_type=jnp.float32).astype(jnp.bfloat16)
    down_running = jnp.zeros((FF, D), jnp.float32)
    up_running = jnp.zeros((D, FF), jnp.float32)
    for member in range(N_WA):
        low = member * TOK_DEV
        high = low + TOK_DEV
        down_running = down_running + rounded(jnp.dot(activated[low:high].T, out_grad[low:high], preferred_element_type=jnp.float32))
        up_running = up_running + rounded(jnp.dot(inputs[low:high].T, hidden_grad[low:high], preferred_element_type=jnp.float32))
    return input_grad, up_running.astype(jnp.bfloat16), down_running.astype(jnp.bfloat16)
```

```python
import jax
import jax.numpy as jnp
from jax import lax
from jax.sharding import PartitionSpec as P


def gelu_parts(values):
    floats = values.astype(jnp.float32)
    square = floats * floats
    inner = 0.7978845608 * (floats + 0.044715 * floats * square)
    tangent = jnp.tanh(inner)
    activated = 0.5 * floats * (1.0 + tangent)
    derivative = 0.5 * (1.0 + tangent) + 0.5 * floats * (1.0 - tangent * tangent) * 0.7978845608 * (
        1.0 + 0.134145 * square
    )
    return (activated, derivative)


def per_device(inputs, out_grad, preact, up_weight, down_weight):
    n_wa = lax.axis_size("wa")
    rows = inputs.shape[0]
    grad = lax.all_gather(out_grad, "ao", axis=1, tiled=True)
    grad = lax.all_gather(grad, "wa", axis=0, tiled=True)
    tokens = lax.all_gather(inputs, "ao", axis=1, tiled=True)
    tokens = lax.all_gather(tokens, "wa", axis=0, tiled=True)
    pre = lax.all_to_all(preact, "wa", split_axis=1, concat_axis=0, tiled=True)
    activated, derivative = gelu_parts(pre)
    activated = activated.astype(jnp.bfloat16)
    partial = jnp.einsum("td,fd->tf", grad, down_weight, preferred_element_type=jnp.float32)
    act_grad = lax.psum(partial.astype(jnp.bfloat16), "ia").astype(jnp.float32)
    hidden_grad = (act_grad * derivative).astype(jnp.bfloat16)
    down_grad = jnp.einsum(
        "tf,td->fd", activated, grad, preferred_element_type=jnp.float32
    ).astype(jnp.bfloat16)
    up_grad = jnp.einsum(
        "td,tf->df", tokens, hidden_grad, preferred_element_type=jnp.float32
    ).astype(jnp.bfloat16)
    term = jnp.einsum("tf,df->td", hidden_grad, up_weight, preferred_element_type=jnp.float32)
    term = lax.psum_scatter(term.astype(jnp.bfloat16), "wa", scatter_dimension=0, tiled=True)
    input_grad = lax.psum_scatter(term, "ao", scatter_dimension=1, tiled=True)
    return (input_grad, up_grad, down_grad)


def solution(mesh):
    placed = (
        P("wa", ("ia", "ao")),
        P("wa", ("ia", "ao")),
        P("wa", "ao"),
        P("ia", ("ao", "wa")),
        P(("ao", "wa"), "ia"),
    )
    return jax.shard_map(
        per_device,
        mesh=mesh,
        in_specs=placed,
        out_specs=(P("wa", ("ia", "ao")), P("ia", ("ao", "wa")), P(("ao", "wa"), "ia")),
        check_vma=False,
    )
```

```python
import jax
import jax.numpy as jnp
from jax import lax
from jax.experimental import pallas as pl
from jax.experimental.pallas import tpu as pltpu
from jax.sharding import PartitionSpec as P

MESH = pl.DeviceIdType.MESH
BF = jnp.bfloat16
F32 = jnp.float32
TOK = 320
FEAT = 192
BLK = 480
DI = 1536
HI = 768
NT = (((1,), (1,)), ((), ()))
TN = (((0,), (0,)), ((), ()))
FWD = (0, 3)


def gelu(u):
    square = u * u
    t = jnp.tanh(0.7978845608 * (u + 0.044715 * u * square))
    return 0.5 * u * (1.0 + t)


def slope(u):
    square = u * u
    t = jnp.tanh(0.7978845608 * (u + 0.044715 * u * square))
    return 0.5 * (1.0 + t) + 0.5 * u * (1.0 - t * t) * 0.7978845608 * (1.0 + 0.134145 * square)


def swap_halves(v):
    return pltpu.roll(v, 64, 1)


def low_lanes(shape):
    return lax.broadcasted_iota(jnp.int32, shape, 1) < 64


def loop(n, body):
    def step(i, carry):
        body(i)
        return carry

    lax.fori_loop(0, n, step, 0)


def kernel(
    grad_in, tok_in, preact, up_w, down_w,
    ig_out, ug_out, dg_out,
    cg, cx, ci, rs, g, xt, wd, wu, par, rc, r1, r2, s1, s2, pre, stage, act, hid, ug, dg,
    ag_send, ag_recv, rs_send, rs_recv, f_send, f_recv, p_send, p_recv, l_sem,
):
    ia, y, ao = lax.axis_index("ia"), lax.axis_index("wa"), lax.axis_index("ao")
    zl, c = ia // 2, ia % 2
    zh, x = ao // 4, ao % 4
    b0, b1 = zl % 2, zl // 2

    def dev(dx=0, dy=0, flip_zh=False, to_zl=None, flip_c=False):
        x_, y_ = (x + dx) % 4, (y + dy) % 4
        zh_ = 1 - zh if flip_zh else zh
        zl_ = zl if to_zl is None else to_zl
        c_ = 1 - c if flip_c else c
        return {"ia": zl_ * 2 + c_, "wa": y_, "ao": zh_ * 4 + x_}

    def dev_p(d):
        return dev(dx=d * (1 - c), dy=d * c)

    def dev_s(d):
        return dev(dx=d * c, dy=d * (1 - c))

    sibling = dev(flip_c=True)
    far_z = dev(flip_zh=True)
    zl1 = dev(to_zl=zl + 1 - 2 * b0)
    zl2 = dev(to_zl=zl + 2 - 4 * b1)

    sent = []

    def push(src, dst, ssem, rsem, to):
        copy = pltpu.make_async_remote_copy(
            src_ref=src, dst_ref=dst, send_sem=ssem, recv_sem=rsem, device_id=to, device_id_type=MESH
        )
        copy.start()
        sent.append(copy)

    def got(dst, rsem, frm):
        pltpu.make_async_remote_copy(
            src_ref=dst, dst_ref=dst, send_sem=l_sem.at[7], recv_sem=rsem, device_id=frm, device_id_type=MESH
        ).wait_recv()

    copies = [
        pltpu.make_async_copy(down_w, wd, l_sem.at[0]),
        pltpu.make_async_copy(up_w, wu, l_sem.at[1]),
        pltpu.make_async_copy(
            preact.at[:, pl.ds(pl.multiple_of(y * HI, 128), HI)], pre.at[0], l_sem.at[2]
        ),
    ]
    for copy in copies:
        copy.start()

    def slot(w, j, k, jr=None, kr=None):
        jr, kr = (j if jr is None else jr), (k if kr is None else kr)
        dx, dy = j + (k - j) * c, kr + (jr - kr) * c
        zh_ = 1 - zh if w else zh
        return dy * 8 + zh_ * 4 + (x + dx) % 4

    def pack(src, dst):
        own = slot(0, 0, 0)

        @pl.when(x % 2 == 0)
        def _():
            v = src[...].astype(F32)
            dst[own, 0:TOK, :] = v[:, 0:128].astype(BF)
            m = v[:, 128:192]
            dst[own, TOK:BLK, :] = jnp.concatenate([m[0:160], m[160:320]], axis=1).astype(BF)

        @pl.when(x % 2 == 1)
        def _():
            v = src[...].astype(F32)
            dst[own, 0:TOK, :] = v[:, 64:192].astype(BF)
            m = v[:, 0:64]
            dst[own, TOK:BLK, :] = jnp.concatenate([m[160:320], m[0:160]], axis=1).astype(BF)

    def unpack(src, dst, r):
        def body(n):
            e = src.at[r * 8 + 2 * n]
            o = src.at[r * 8 + 2 * n + 1]
            rows = pl.ds(r * TOK, TOK)
            base = n * 384
            dst[rows, pl.ds(pl.multiple_of(base, 128), 128)] = e[0:TOK, :]
            dst[rows, pl.ds(pl.multiple_of(base + 256, 128), 128)] = o[0:TOK, :]
            p, q = e[TOK:BLK, :].astype(F32), o[TOK:BLK, :].astype(F32)
            low = low_lanes((160, 128))
            mid = pl.ds(pl.multiple_of(base + 128, 128), 128)
            dst[pl.ds(r * TOK, 160), mid] = jnp.where(low, p, q).astype(BF)
            dst[pl.ds(r * TOK + 160, 160), mid] = swap_halves(jnp.where(low, q, p)).astype(BF)

        loop(4, body)

    pack(grad_in, cg)
    pack(tok_in, cx)

    barrier = pltpu.get_barrier_semaphore()
    partners = [dev_p(1), dev_p(3), dev_s(1), dev_s(3), dev(dy=2), sibling, far_z, zl1, zl2]
    for partner in partners[0:4] + partners[5:]:
        pl.semaphore_signal(barrier, inc=1, device_id=partner, device_id_type=MESH)
    pl.semaphore_wait(barrier, 8)

    class Gather:
        def __init__(self, index, buf):
            self.index, self.buf, self.n, self.have = index, buf, 0, {(0, 0, 0)}

        def _push(self, w, j, k, jr, kr, to, wr=None):
            push(
                self.buf.at[slot(w, j, k)],
                self.buf.at[slot(w, j, k, jr, kr)],
                ag_send.at[self.index, self.n],
                ag_recv.at[self.index, w if wr is None else wr, jr, kr],
                to,
            )
            self.n += 1

        def p(self, w, j, d):
            self._push(w, j, 0, (j - d) % 4, 0, dev_p(d))

        def s(self, w, j, k, d):
            self._push(w, j, k, j, (k - d) % 4, dev_s(d))

        def far(self):
            self._push(0, 0, 0, 0, 0, far_z, wr=1)

        def get(self, w, j, k):
            if (w, j, k) in self.have:
                return
            self.have.add((w, j, k))
            got(self.buf.at[slot(w, j, k)], ag_recv.at[self.index, w, j, k], dev_p(1))
            if k == 0:
                if j == 0:
                    self.start(w)
                    return
                if w == 0 and j == 3:
                    self.p(w, j, 1)
                if w == 1 and j == 1:
                    self.p(w, j, 3)
                self.s(w, j, k, 1)
                self.s(w, j, k, 3)
            elif k == 3 and j in FWD:
                self.s(w, j, k, 1)
            elif k == 1 and j not in FWD:
                self.s(w, j, k, 3)

        def start(self, w):
            for d in (1, 3):
                self.p(w, 0, d)
                self.s(w, 0, 0, d)

        def tokens(self, r):
            for w in (0, 1):
                for i in (0, 1, 3, 2):
                    self.get(w, i, r)
                for i in (0, 1, 3, 2):
                    self.get(w, r, i)

    grad, tok = Gather(0, cg), Gather(1, cx)

    half = pl.ds(pl.multiple_of(c * 160, 16), 160)
    other = pl.ds(pl.multiple_of((1 - c) * 160, 16), 160)
    up = 1 + 2 * c

    def preact_send():
        def cols(d):
            return pl.ds(pl.multiple_of(((y + d) % 4) * HI, 128), HI)

        push(preact.at[half, cols(2)], stage, p_send.at[0], p_recv.at[0], dev(dy=up))
        for d in (1, 3):
            push(preact.at[half, cols(d)], pre.at[4 - d, half], p_send.at[d], p_recv.at[4 - d], dev(dy=d))

    def preact_relay():
        got(stage, p_recv.at[0], dev(dy=1))
        push(stage, pre.at[2, half], p_send.at[2], p_recv.at[2], dev(dy=up))

    def preact_get(r):
        got(pre.at[r, half], p_recv.at[r], dev(dy=1))
        push(pre.at[r, half], pre.at[r, half], p_send.at[3 + r], p_recv.at[3 + r], sibling)

    def activate(r):
        if r > 0:
            got(pre.at[r, other], p_recv.at[3 + r], sibling)

        def body(i):
            rows = pl.multiple_of(i * 32, 32)
            u = pre[r, pl.ds(rows, 32), :].astype(F32)
            act[pl.ds(r * TOK + rows, 32), :] = gelu(u).astype(BF)

        loop(10, body)

    rows80 = pl.ds(pl.multiple_of(c * 160 + b0 * 80, 16), 80)
    keep80, give80 = pl.ds(pl.multiple_of(b0 * 80, 16), 80), pl.ds(pl.multiple_of((1 - b0) * 80, 16), 80)
    peer80 = pl.ds(pl.multiple_of(c * 160 + (1 - b0) * 80, 16), 80)
    keep384 = pl.ds(pl.multiple_of(b1 * 384, 128), 384)
    give384 = pl.ds(pl.multiple_of((1 - b1) * 384, 128), 384)

    def f1(r):
        grad.tokens(r)
        unpack(cg, g, r)
        if r == 0:
            copies[0].wait()

        def body(n):
            cols = pl.ds(pl.multiple_of(n * 256, 256), 256)
            par[r, :, cols] = lax.dot_general(
                g[r * TOK:(r + 1) * TOK, :], wd[cols, :], NT, preferred_element_type=F32
            ).astype(BF)

        loop(3, body)
        push(par.at[r, other], rc.at[r], f_send.at[0, r], f_recv.at[0, r], sibling)

    def f2(r):
        got(rc.at[r], f_recv.at[0, r], sibling)
        s1[r] = (par[r, half, :].astype(F32) + rc[r].astype(F32)).astype(BF)
        push(s1.at[r, give80], r1.at[r], f_send.at[1, r], f_recv.at[1, r], zl1)

    def f3(r):
        got(r1.at[r], f_recv.at[1, r], zl1)
        s2[r] = (s1[r, keep80, :].astype(F32) + r1[r].astype(F32)).astype(BF)
        push(s2.at[r, :, give384], r2.at[r], f_send.at[2, r], f_recv.at[2, r], zl2)

    def hrows(r, ds):
        return pl.ds(pl.multiple_of(r * TOK + ds.start, 16), ds.size)

    def f4(r):
        if r == 0:
            copies[2].wait()
        got(r2.at[r], f_recv.at[2, r], zl2)
        total = s2[r, :, keep384].astype(F32) + r2[r].astype(F32)
        u = pre[r, rows80, keep384].astype(F32)
        hid[hrows(r, rows80), keep384] = (total * slope(u)).astype(BF)
        piece = hid.at[hrows(r, rows80), keep384]
        push(piece, piece, f_send.at[3, r], f_recv.at[3, r], zl2)

    def f5(r):
        got(hid.at[hrows(r, rows80), give384], f_recv.at[3, r], zl2)
        piece = hid.at[hrows(r, rows80), :]
        push(piece, piece, f_send.at[4, r], f_recv.at[4, r], zl1)

    def f6(r):
        got(hid.at[hrows(r, peer80), :], f_recv.at[4, r], zl1)
        piece = hid.at[hrows(r, half), :]
        push(piece, piece, f_send.at[5, r], f_recv.at[5, r], sibling)

    def f7(r):
        got(hid.at[hrows(r, other), :], f_recv.at[5, r], sibling)
        if r == 0:
            copies[1].wait()

        def body(n):
            cols = pl.ds(pl.multiple_of(n * 384, 128), 384)
            term = lax.dot_general(
                hid[r * TOK:(r + 1) * TOK, :], wu[cols, :], NT, preferred_element_type=F32
            )
            even, odd = r * 8 + 2 * n, r * 8 + 2 * n + 1
            ci[even, 0:TOK, :] = term[:, 0:128].astype(BF)
            ci[odd, 0:TOK, :] = term[:, 256:384].astype(BF)
            top, bot = term[0:160, 128:256], swap_halves(term[160:320, 128:256])
            low = low_lanes((160, 128))
            ci[even, TOK:BLK, :] = jnp.where(low, top, bot).astype(BF)
            ci[odd, TOK:BLK, :] = jnp.where(low, bot, top).astype(BF)

        loop(4, body)

    def down(lo, hi):
        def body(i):
            cols = pl.ds(pl.multiple_of((lo + i) * 256, 256), 256)
            dg[:, cols] = lax.dot_general(act[...], g[:, cols], TN, preferred_element_type=F32).astype(BF)

        loop(hi - lo, body)

    def upg(lo, hi):
        def body(i):
            cols = pl.ds(pl.multiple_of((lo + i) * 256, 256), 256)
            ug[cols, :] = lax.dot_general(xt[:, cols], hid[...], TN, preferred_element_type=F32).astype(BF)

        loop(hi - lo, body)

    rs_count = []

    def rs_push(block, index, to):
        push(ci.at[block], rs.at[index], rs_send.at[index], rs_recv.at[index], to)

    def rs_add(block, *indices):
        total = ci[block].astype(F32)
        for index in indices:
            got(rs.at[index], rs_recv.at[index], dev_p(1))
            total = total + rs[index].astype(F32)
        return total

    def s_open(w, j):
        d, base = (1 if j in FWD else 3), (w * 4 + j) * 3
        rs_push(slot(w, j, 2), base, dev_s(d))
        rs_push(slot(w, j, 4 - d), base + 2, dev_s(4 - d))

    def s_mid(w, j):
        d, base = (1 if j in FWD else 3), (w * 4 + j) * 3
        block = slot(w, j, d)
        ci[block] = rs_add(block, base).astype(BF)
        rs_push(block, base + 1, dev_s(d))

    def s_end(w, j):
        base = (w * 4 + j) * 3
        block = slot(w, j, 0)
        ci[block] = rs_add(block, base + 1, base + 2).astype(BF)

    def p_open(w, j):
        d, base = (3 if w else 1), 24 + w * 3
        rs_push(slot(w, j, 0), base + (0 if j == 2 else 2), dev_p(d if j == 2 else 4 - d))

    def p_mid(w):
        d, base = (3 if w else 1), 24 + w * 3
        block = slot(w, d, 0)
        ci[block] = rs_add(block, base).astype(BF)
        rs_push(block, base + 1, dev_p(d))

    def p_end(w):
        base = 24 + w * 3
        block = slot(w, 0, 0)
        ci[block] = rs_add(block, base + 1, base + 2).astype(BF)
        if w:
            rs_push(block, 30, far_z)

    grad.far()
    grad.start(0)
    for key in ((0, 3, 0), (0, 1, 0), (0, 0, 3), (0, 0, 1), (0, 2, 0), (0, 1, 1), (0, 3, 3)):
        grad.get(*key)
    grad.get(1, 0, 0)
    tok.far()
    preact_send()
    for key in ((0, 2, 1), (0, 1, 3), (0, 3, 1), (0, 2, 3), (1, 3, 0), (1, 1, 0), (1, 0, 3), (1, 0, 1), (1, 2, 0)):
        grad.get(*key)
    f1(0)
    for key in ((1, 1, 1), (1, 3, 3), (1, 2, 1)):
        grad.get(*key)
    tok.start(0)
    f2(0)
    preact_relay()
    preact_get(1)
    preact_get(3)
    f1(1)
    f3(0)
    f1(3)
    f2(1)
    f4(0)
    tok.get(0, 3, 0)
    tok.get(0, 1, 0)
    f1(2)
    f2(3)
    f3(1)
    preact_get(2)
    f5(0)
    for key in ((0, 0, 3), (0, 0, 1), (1, 0, 0)):
        tok.get(*key)
    f2(2)
    f3(3)
    f4(1)
    f6(0)
    for key in ((0, 2, 0), (0, 1, 1), (0, 3, 3)):
        tok.get(*key)
    activate(0)
    f5(1)
    f3(2)
    f4(3)
    f7(0)
    for key in ((1, 3, 0), (1, 1, 0), (1, 0, 3), (1, 0, 1), (0, 2, 1)):
        tok.get(*key)
    f6(1)
    activate(1)
    f5(3)
    f4(2)
    f7(1)
    for key in ((1, 2, 0), (1, 1, 1), (1, 3, 3), (1, 2, 1)):
        tok.get(*key)
    activate(3)
    f6(3)
    f5(2)
    activate(2)
    f7(3)
    tok.tokens(0)
    f6(2)
    down(0, 3)
    f7(2)
    for j in (2, 1, 3, 0):
        s_open(1, j)
    down(3, 6)
    dg_copy = pltpu.make_async_copy(dg, dg_out, l_sem.at[3])
    dg_copy.start()
    for j in (2, 1, 3, 0):
        s_open(0, j)
    for j in (2, 1, 3, 0):
        s_mid(1, j)
    for r in (0, 1, 3, 2):
        tok.tokens(r)
    s_end(1, 2)
    p_open(1, 2)
    s_end(1, 1)
    p_open(1, 1)
    s_end(1, 3)
    p_mid(1)
    s_mid(0, 2)
    s_mid(0, 1)
    s_mid(0, 3)
    s_mid(0, 0)
    s_end(1, 0)
    p_end(1)
    for r in (0, 1, 2, 3):
        unpack(cx, xt, r)
    s_end(0, 2)
    p_open(0, 2)
    s_end(0, 3)
    p_open(0, 3)
    s_end(0, 1)
    upg(0, 2)
    p_mid(0)
    upg(2, 6)
    ug_copy = pltpu.make_async_copy(ug, ug_out, l_sem.at[4])
    ug_copy.start()
    s_end(0, 0)
    p_end(0)
    total = rs_add(slot(0, 0, 0), 30)
    mini = total[TOK:BLK, :]

    @pl.when(x % 2 == 0)
    def _():
        ig_out[:, 0:128] = total[0:TOK].astype(BF)
        ig_out[0:160, 128:192] = mini[:, 0:64].astype(BF)
        ig_out[160:320, 128:192] = mini[:, 64:128].astype(BF)

    @pl.when(x % 2 == 1)
    def _():
        ig_out[160:320, :] = jnp.concatenate([mini[:, 0:64], total[160:TOK]], axis=1).astype(BF)
        ig_out[0:160, :] = jnp.concatenate([mini[:, 64:128], total[0:160]], axis=1).astype(BF)

    dg_copy.wait()
    ug_copy.wait()
    for copy in sent:
        copy.wait_send()


def per_device(inputs, out_grad, preact, up_weight, down_weight):
    vmem = pl.BlockSpec(memory_space=pltpu.VMEM)
    hbm = pl.BlockSpec(memory_space=pl.ANY)
    blocks = pltpu.VMEM((32, BLK, 128), BF)
    dma = pltpu.SemaphoreType.DMA
    tokens = 4 * TOK
    return pl.pallas_call(
        kernel,
        out_shape=(
            jax.ShapeDtypeStruct((TOK, FEAT), BF),
            jax.ShapeDtypeStruct((DI, HI), BF),
            jax.ShapeDtypeStruct((HI, DI), BF),
        ),
        in_specs=[vmem, vmem, hbm, hbm, hbm],
        out_specs=(vmem, hbm, hbm),
        scratch_shapes=[
            blocks, blocks, blocks,
            pltpu.VMEM((31, BLK, 128), BF),
            pltpu.VMEM((tokens, DI), BF),
            pltpu.VMEM((tokens, DI), BF),
            pltpu.VMEM((HI, DI), BF),
            pltpu.VMEM((DI, HI), BF),
            pltpu.VMEM((4, TOK, HI), BF),
            pltpu.VMEM((4, 160, HI), BF),
            pltpu.VMEM((4, 80, HI), BF),
            pltpu.VMEM((4, 80, 384), BF),
            pltpu.VMEM((4, 160, HI), BF),
            pltpu.VMEM((4, 80, HI), BF),
            pltpu.VMEM((4, TOK, HI), BF),
            pltpu.VMEM((160, HI), BF),
            pltpu.VMEM((tokens, HI), BF),
            pltpu.VMEM((tokens, HI), BF),
            pltpu.VMEM((DI, HI), BF),
            pltpu.VMEM((HI, DI), BF),
            dma((2, 31)), dma((2, 2, 4, 4)),
            dma((31,)), dma((31,)),
            dma((6, 4)), dma((6, 4)),
            dma((7,)), dma((7,)),
            dma((8,)),
        ],
        compiler_params=pltpu.CompilerParams(
            collective_id=0, has_side_effects=True, vmem_limit_bytes=62 * 1024 * 1024
        ),
        name="ffn_backward",
    )(out_grad, inputs, preact, up_weight, down_weight)


def solution(mesh):
    placed = (
        P("wa", ("ia", "ao")),
        P("wa", ("ia", "ao")),
        P("wa", "ao"),
        P("ia", ("ao", "wa")),
        P(("ao", "wa"), "ia"),
    )
    return jax.shard_map(
        per_device,
        mesh=mesh,
        in_specs=placed,
        out_specs=(P("wa", ("ia", "ao")), P("ia", ("ao", "wa")), P(("ao", "wa"), "ia")),
        check_vma=False,
    )
```

```python
import jax
import jax.numpy as jnp
from jax import lax
from jax.experimental import pallas as pl
from jax.experimental.pallas import tpu as pltpu
from jax.sharding import PartitionSpec as P

MESH = pl.DeviceIdType.MESH
BF = jnp.bfloat16
F32 = jnp.float32
TOK = 320
FEAT = 192
BLK = 480
DI = 1536
HI = 768
NT = (((1,), (1,)), ((), ()))
TN = (((0,), (0,)), ((), ()))
FWD = (0, 3)


def gelu(u):
    square = u * u
    t = jnp.tanh(0.7978845608 * (u + 0.044715 * u * square))
    return 0.5 * u * (1.0 + t)


def slope(u):
    square = u * u
    t = jnp.tanh(0.7978845608 * (u + 0.044715 * u * square))
    return 0.5 * (1.0 + t) + 0.5 * u * (1.0 - t * t) * 0.7978845608 * (1.0 + 0.134145 * square)


def swap_halves(v):
    return pltpu.roll(v, 64, 1)


def low_lanes(shape):
    return lax.broadcasted_iota(jnp.int32, shape, 1) < 64


def loop(n, body):
    def step(i, carry):
        body(i)
        return carry

    lax.fori_loop(0, n, step, 0)


def kernel(
    grad_in, tok_in, preact, up_w, down_w,
    ig_out, ug, dg,
    cg, cx, ci, rs, g, xt, wd, wu, par, rc, r1, r2, s1, s2, pre, stage, act, hid,
    ag_send, ag_recv, rs_send, rs_recv, f_send, f_recv, p_send, p_recv, l_sem,
):
    ia, y, ao = lax.axis_index("ia"), lax.axis_index("wa"), lax.axis_index("ao")
    zl, c = ia // 2, ia % 2
    zh, x = ao // 4, ao % 4
    b0, b1 = zl % 2, zl // 2

    def dev(dx=0, dy=0, flip_zh=False, to_zl=None, flip_c=False):
        x_, y_ = (x + dx) % 4, (y + dy) % 4
        zh_ = 1 - zh if flip_zh else zh
        zl_ = zl if to_zl is None else to_zl
        c_ = 1 - c if flip_c else c
        return {"ia": zl_ * 2 + c_, "wa": y_, "ao": zh_ * 4 + x_}

    def dev_p(d):
        return dev(dx=d * (1 - c), dy=d * c)

    def dev_s(d):
        return dev(dx=d * c, dy=d * (1 - c))

    sibling = dev(flip_c=True)
    far_z = dev(flip_zh=True)
    zl1 = dev(to_zl=zl + 1 - 2 * b0)
    zl2 = dev(to_zl=zl + 2 - 4 * b1)

    sent = []

    def push(src, dst, ssem, rsem, to):
        copy = pltpu.make_async_remote_copy(
            src_ref=src, dst_ref=dst, send_sem=ssem, recv_sem=rsem, device_id=to, device_id_type=MESH
        )
        copy.start()
        sent.append(copy)

    def got(dst, rsem, frm):
        pltpu.make_async_remote_copy(
            src_ref=dst, dst_ref=dst, send_sem=l_sem.at[7], recv_sem=rsem, device_id=frm, device_id_type=MESH
        ).wait_recv()

    copies = [
        pltpu.make_async_copy(down_w, wd, l_sem.at[0]),
        pltpu.make_async_copy(up_w, wu, l_sem.at[1]),
        pltpu.make_async_copy(
            preact.at[:, pl.ds(pl.multiple_of(y * HI, 128), HI)], pre.at[0], l_sem.at[2]
        ),
    ]
    for copy in copies:
        copy.start()

    def slot(w, j, k, jr=None, kr=None):
        jr, kr = (j if jr is None else jr), (k if kr is None else kr)
        dx, dy = j + (k - j) * c, kr + (jr - kr) * c
        zh_ = 1 - zh if w else zh
        return dy * 8 + zh_ * 4 + (x + dx) % 4

    def pack(src, dst):
        own = slot(0, 0, 0)

        def place(main, mini, first, second):
            dst[own, 0:TOK, :] = src[main:main + 128, :].astype(F32).T.astype(BF)
            m = src[mini:mini + 64, :].astype(F32).T
            halves = (m[0:160], m[160:320])
            dst[own, TOK:BLK, :] = jnp.concatenate([halves[first], halves[second]], axis=1).astype(BF)

        @pl.when(x % 2 == 0)
        def _():
            place(0, 128, 0, 1)

        @pl.when(x % 2 == 1)
        def _():
            place(64, 0, 1, 0)

    def unpack(src, dst, r):
        def body(n):
            e = src.at[r * 8 + 2 * n]
            o = src.at[r * 8 + 2 * n + 1]
            rows = pl.ds(r * TOK, TOK)
            base = n * 384
            dst[rows, pl.ds(pl.multiple_of(base, 128), 128)] = e[0:TOK, :]
            dst[rows, pl.ds(pl.multiple_of(base + 256, 128), 128)] = o[0:TOK, :]
            p, q = e[TOK:BLK, :].astype(F32), o[TOK:BLK, :].astype(F32)
            low = low_lanes((160, 128))
            mid = pl.ds(pl.multiple_of(base + 128, 128), 128)
            dst[pl.ds(r * TOK, 160), mid] = jnp.where(low, p, q).astype(BF)
            dst[pl.ds(r * TOK + 160, 160), mid] = swap_halves(jnp.where(low, q, p)).astype(BF)

        loop(4, body)

    pack(grad_in, cg)
    pack(tok_in, cx)

    barrier = pltpu.get_barrier_semaphore()
    partners = [dev_p(1), dev_p(3), dev_s(1), dev_s(3), dev(dy=2), sibling, far_z, zl1, zl2]
    for partner in partners[0:4] + partners[5:]:
        pl.semaphore_signal(barrier, inc=1, device_id=partner, device_id_type=MESH)
    pl.semaphore_wait(barrier, 8)

    class Gather:
        def __init__(self, index, buf):
            self.index, self.buf, self.n, self.have = index, buf, 0, {(0, 0, 0)}

        def _push(self, w, j, k, jr, kr, to, wr=None):
            push(
                self.buf.at[slot(w, j, k)],
                self.buf.at[slot(w, j, k, jr, kr)],
                ag_send.at[self.index, self.n],
                ag_recv.at[self.index, w if wr is None else wr, jr, kr],
                to,
            )
            self.n += 1

        def p(self, w, j, d):
            self._push(w, j, 0, (j - d) % 4, 0, dev_p(d))

        def s(self, w, j, k, d):
            self._push(w, j, k, j, (k - d) % 4, dev_s(d))

        def far(self):
            self._push(0, 0, 0, 0, 0, far_z, wr=1)

        def get(self, w, j, k):
            if (w, j, k) in self.have:
                return
            self.have.add((w, j, k))
            got(self.buf.at[slot(w, j, k)], ag_recv.at[self.index, w, j, k], dev_p(1))
            if k == 0:
                if j == 0:
                    self.start(w)
                    return
                if w == 0 and j == 3:
                    self.p(w, j, 1)
                if w == 1 and j == 1:
                    self.p(w, j, 3)
                self.s(w, j, k, 1)
                self.s(w, j, k, 3)
            elif k == 3 and j in FWD:
                self.s(w, j, k, 1)
            elif k == 1 and j not in FWD:
                self.s(w, j, k, 3)

        def start(self, w):
            for d in (1, 3):
                self.p(w, 0, d)
                self.s(w, 0, 0, d)

        def tokens(self, r):
            for w in (0, 1):
                for i in (0, 1, 3, 2):
                    self.get(w, i, r)
                for i in (0, 1, 3, 2):
                    self.get(w, r, i)

    grad, tok = Gather(0, cg), Gather(1, cx)

    half = pl.ds(pl.multiple_of(c * 160, 16), 160)
    other = pl.ds(pl.multiple_of((1 - c) * 160, 16), 160)
    up = 1 + 2 * c

    def preact_send():
        def cols(d):
            return pl.ds(pl.multiple_of(((y + d) % 4) * HI, 128), HI)

        push(preact.at[half, cols(2)], stage, p_send.at[0], p_recv.at[0], dev(dy=up))
        for d in (1, 3):
            push(preact.at[half, cols(d)], pre.at[4 - d, half], p_send.at[d], p_recv.at[4 - d], dev(dy=d))

    def preact_relay():
        got(stage, p_recv.at[0], dev(dy=1))
        push(stage, pre.at[2, half], p_send.at[2], p_recv.at[2], dev(dy=up))

    def preact_get(r):
        got(pre.at[r, half], p_recv.at[r], dev(dy=1))
        push(pre.at[r, half], pre.at[r, half], p_send.at[3 + r], p_recv.at[3 + r], sibling)

    def activate(r):
        if r > 0:
            got(pre.at[r, other], p_recv.at[3 + r], sibling)

        def body(i):
            rows = pl.multiple_of(i * 32, 32)
            u = pre[r, pl.ds(rows, 32), :].astype(F32)
            act[pl.ds(r * TOK + rows, 32), :] = gelu(u).astype(BF)

        loop(10, body)

    rows80 = pl.ds(pl.multiple_of(c * 160 + b0 * 80, 16), 80)
    keep80, give80 = pl.ds(pl.multiple_of(b0 * 80, 16), 80), pl.ds(pl.multiple_of((1 - b0) * 80, 16), 80)
    peer80 = pl.ds(pl.multiple_of(c * 160 + (1 - b0) * 80, 16), 80)
    keep384 = pl.ds(pl.multiple_of(b1 * 384, 128), 384)
    give384 = pl.ds(pl.multiple_of((1 - b1) * 384, 128), 384)

    def f1(r):
        grad.tokens(r)
        unpack(cg, g, r)
        if r == 0:
            copies[0].wait()

        def body(n):
            cols = pl.ds(pl.multiple_of(n * 256, 256), 256)
            par[r, :, cols] = lax.dot_general(
                g[r * TOK:(r + 1) * TOK, :], wd[cols, :], NT, preferred_element_type=F32
            ).astype(BF)

        loop(3, body)
        push(par.at[r, other], rc.at[r], f_send.at[0, r], f_recv.at[0, r], sibling)

    def f2(r):
        got(rc.at[r], f_recv.at[0, r], sibling)
        s1[r] = (par[r, half, :].astype(F32) + rc[r].astype(F32)).astype(BF)
        push(s1.at[r, give80], r1.at[r], f_send.at[1, r], f_recv.at[1, r], zl1)

    def f3(r):
        got(r1.at[r], f_recv.at[1, r], zl1)
        s2[r] = (s1[r, keep80, :].astype(F32) + r1[r].astype(F32)).astype(BF)
        push(s2.at[r, :, give384], r2.at[r], f_send.at[2, r], f_recv.at[2, r], zl2)

    def hrows(r, ds):
        return pl.ds(pl.multiple_of(r * TOK + ds.start, 16), ds.size)

    def f4(r):
        got(r2.at[r], f_recv.at[2, r], zl2)
        total = s2[r, :, keep384].astype(F32) + r2[r].astype(F32)
        u = pre[r, rows80, keep384].astype(F32)
        hid[hrows(r, rows80), keep384] = (total * slope(u)).astype(BF)
        piece = hid.at[hrows(r, rows80), keep384]
        push(piece, piece, f_send.at[3, r], f_recv.at[3, r], zl2)

    def f5(r):
        got(hid.at[hrows(r, rows80), give384], f_recv.at[3, r], zl2)
        piece = hid.at[hrows(r, rows80), :]
        push(piece, piece, f_send.at[4, r], f_recv.at[4, r], zl1)

    def f6(r):
        got(hid.at[hrows(r, peer80), :], f_recv.at[4, r], zl1)
        piece = hid.at[hrows(r, half), :]
        push(piece, piece, f_send.at[5, r], f_recv.at[5, r], sibling)

    def f7(r):
        got(hid.at[hrows(r, other), :], f_recv.at[5, r], sibling)
        if r == 0:
            copies[1].wait()

        def body(n):
            cols = pl.ds(pl.multiple_of(n * 384, 128), 384)
            term = lax.dot_general(
                hid[r * TOK:(r + 1) * TOK, :], wu[cols, :], NT, preferred_element_type=F32
            )
            even, odd = r * 8 + 2 * n, r * 8 + 2 * n + 1
            ci[even, 0:TOK, :] = term[:, 0:128].astype(BF)
            ci[odd, 0:TOK, :] = term[:, 256:384].astype(BF)
            top, bot = term[0:160, 128:256], swap_halves(term[160:320, 128:256])
            low = low_lanes((160, 128))
            ci[even, TOK:BLK, :] = jnp.where(low, top, bot).astype(BF)
            ci[odd, TOK:BLK, :] = jnp.where(low, bot, top).astype(BF)

        loop(4, body)

    def down(lo, hi):
        def body(i):
            cols = pl.ds(pl.multiple_of((lo + i) * 256, 256), 256)
            dg[:, cols] = lax.dot_general(act[...], g[:, cols], TN, preferred_element_type=F32).astype(BF)

        loop(hi - lo, body)

    def upg(lo, hi):
        def body(i):
            cols = pl.ds(pl.multiple_of((lo + i) * 256, 256), 256)
            ug[cols, :] = lax.dot_general(xt[:, cols], hid[...], TN, preferred_element_type=F32).astype(BF)

        loop(hi - lo, body)

    def rs_push(block, index, to):
        pltpu.make_async_remote_copy(
            src_ref=ci.at[block], dst_ref=rs.at[index], send_sem=rs_send.at[index], recv_sem=rs_recv.at[index],
            device_id=to, device_id_type=MESH,
        ).start()

    def rs_add(block, *indices):
        total = ci[block].astype(F32)
        for index in indices:
            got(rs.at[index], rs_recv.at[index], dev_p(1))
            total = total + rs[index].astype(F32)
        return total

    def s_far(w, j):
        rs_push(slot(w, j, 2), (w * 4 + j) * 3, dev_s(1 if j in FWD else 3))

    def s_near(w, j):
        d = 3 if j in FWD else 1
        rs_push(slot(w, j, d), (w * 4 + j) * 3 + 2, dev_s(d))

    def s_mid(w, j):
        d, base = (1 if j in FWD else 3), (w * 4 + j) * 3
        block = slot(w, j, d)
        ci[block] = rs_add(block, base).astype(BF)
        rs_push(block, base + 1, dev_s(d))

    def s_end(w, j):
        base = (w * 4 + j) * 3
        block = slot(w, j, 0)
        ci[block] = rs_add(block, base + 1, base + 2).astype(BF)

    def p_open(w, j):
        d, base = (3 if w else 1), 24 + w * 3
        rs_push(slot(w, j, 0), base + (0 if j == 2 else 2), dev_p(d if j == 2 else 4 - d))

    def p_mid(w):
        d, base = (3 if w else 1), 24 + w * 3
        block = slot(w, d, 0)
        ci[block] = rs_add(block, base).astype(BF)
        rs_push(block, base + 1, dev_p(d))

    def p_end(w):
        base = 24 + w * 3
        block = slot(w, 0, 0)
        ci[block] = rs_add(block, base + 1, base + 2).astype(BF)
        if w:
            rs_push(block, 30, far_z)

    def early0(r):
        for w in (1, 0):
            for j in (2, 1, 3, 0):
                if r == 2:
                    s_far(w, j)
                elif r == (3 if j in FWD else 1):
                    s_near(w, j)
                elif r:
                    s_mid(w, j)

    def early1(r):
        last = {0: (), 2: (0,), 1: (2,), 3: (1,)}[r]
        done = {0: (), 2: (), 1: (0,), 3: (2,)}[r]
        for w in (1, 0):
            for j in last:
                s_mid(w, j)
            s_far(w, r)
            s_near(w, r)
        for w in (1, 0):
            for j in done:
                s_end(w, j)
                if j == 2:
                    p_open(w, 2)

    def tail0(part):
        if part < 2:
            w = 1 - part
            near, far = (1, 3) if w else (3, 1)
            s_end(w, 2)
            p_open(w, 2)
            s_end(w, near)
            p_open(w, near)
            s_end(w, far)
            p_mid(w)
        else:
            s_end(3 - part, 0)
            p_end(3 - part)

    def tail1(part):
        if part == 0:
            s_mid(1, 3)
            s_mid(0, 3)
            s_end(1, 1)
            p_open(1, 1)
        elif part == 1:
            s_end(0, 1)
            p_mid(0)
            s_end(1, 3)
            p_mid(1)
        elif part == 2:
            s_end(0, 3)
            p_open(0, 3)
            p_end(1)
        else:
            p_end(0)

    def by_core(first, second, *args):
        @pl.when(c == 0)
        def _():
            first(*args)

        @pl.when(c == 1)
        def _():
            second(*args)

    def early(r):
        by_core(early0, early1, r)

    def gets(gather, *keys):
        for key in keys:
            gather.get(*key)

    grad.far()
    grad.start(0)
    gets(grad, (0, 3, 0), (0, 1, 0), (0, 0, 3), (0, 0, 1), (1, 0, 0))
    gets(grad, (0, 2, 0), (0, 1, 1), (0, 3, 3))
    tok.far()
    gets(grad, (0, 2, 1), (1, 3, 0), (1, 1, 0), (1, 0, 3), (1, 0, 1))
    preact_send()
    gets(grad, (1, 2, 0), (1, 1, 1), (1, 3, 3))
    f1(0)
    gets(grad, (1, 2, 1))
    tok.start(0)
    copies[2].wait()
    activate(0)
    f2(0)
    preact_relay()
    f3(0)
    f1(2)
    preact_get(1)
    preact_get(3)
    f4(0)
    f2(2)
    gets(tok, (0, 3, 0), (0, 1, 0), (0, 0, 3), (0, 0, 1), (1, 0, 0))
    f1(1)
    f5(0)
    f3(2)
    f2(1)
    f1(3)
    preact_get(2)
    f6(0)
    f4(2)
    gets(tok, (0, 2, 0), (0, 1, 1), (0, 3, 3))
    f3(1)
    f2(3)
    f7(0)
    early(0)
    f5(2)
    gets(tok, (0, 2, 1), (1, 3, 0), (1, 1, 0), (1, 0, 3), (1, 0, 1))
    activate(1)
    f4(1)
    f3(3)
    f6(2)
    activate(3)
    f7(2)
    early(2)
    f5(1)
    f4(3)
    gets(tok, (1, 2, 0), (1, 1, 1), (1, 3, 3), (1, 2, 1))
    activate(2)
    down(0, 2)
    f6(1)
    f5(3)
    f7(1)
    early(1)
    down(2, 4)
    f6(3)
    for r in (0, 1):
        tok.tokens(r)
        unpack(cx, xt, r)
    f7(3)
    early(3)
    for r in (3, 2):
        tok.tokens(r)
        unpack(cx, xt, r)
    by_core(tail0, tail1, 0)
    upg(0, 1)
    by_core(tail0, tail1, 1)
    upg(1, 3)
    by_core(tail0, tail1, 2)
    upg(3, 6)
    down(4, 6)
    by_core(tail0, tail1, 3)
    total = rs_add(slot(0, 0, 0), 30)
    main, left, right = total[0:TOK], total[TOK:BLK, 0:64], total[TOK:BLK, 64:128]

    @pl.when(x % 2 == 0)
    def _():
        ig_out[0:128, :] = main.T.astype(BF)
        ig_out[128:192, :] = jnp.concatenate([left, right], axis=0).T.astype(BF)

    @pl.when(x % 2 == 1)
    def _():
        ig_out[64:192, :] = main.T.astype(BF)
        ig_out[0:64, :] = jnp.concatenate([right, left], axis=0).T.astype(BF)

    for copy in sent:
        copy.wait_send()
    for index in range(31):
        pltpu.make_async_remote_copy(
            src_ref=ci.at[0], dst_ref=rs.at[index], send_sem=rs_send.at[index], recv_sem=rs_recv.at[index],
            device_id=far_z, device_id_type=MESH,
        ).wait_send()


def per_device(inputs, out_grad, preact, up_weight, down_weight):
    vmem = pl.BlockSpec(memory_space=pltpu.VMEM)
    hbm = pl.BlockSpec(memory_space=pltpu.HBM)
    blocks = pltpu.VMEM((32, BLK, 128), BF)
    dma = pltpu.SemaphoreType.DMA
    tokens = 4 * TOK
    input_grad, up_grad, down_grad = pl.pallas_call(
        kernel,
        out_shape=(
            jax.ShapeDtypeStruct((FEAT, TOK), BF),
            pltpu.VMEM((DI, HI), BF),
            pltpu.VMEM((HI, DI), BF),
        ),
        in_specs=[vmem, vmem, hbm, hbm, hbm],
        out_specs=(vmem, vmem, vmem),
        scratch_shapes=[
            blocks, blocks, blocks,
            pltpu.VMEM((31, BLK, 128), BF),
            pltpu.VMEM((tokens, DI), BF),
            pltpu.VMEM((tokens, DI), BF),
            pltpu.VMEM((HI, DI), BF),
            pltpu.VMEM((DI, HI), BF),
            pltpu.VMEM((4, TOK, HI), BF),
            pltpu.VMEM((4, 160, HI), BF),
            pltpu.VMEM((4, 80, HI), BF),
            pltpu.VMEM((4, 80, 384), BF),
            pltpu.VMEM((4, 160, HI), BF),
            pltpu.VMEM((4, 80, HI), BF),
            pltpu.VMEM((4, TOK, HI), BF),
            pltpu.VMEM((160, HI), BF),
            pltpu.VMEM((tokens, HI), BF),
            pltpu.VMEM((tokens, HI), BF),
            dma((2, 31)), dma((2, 2, 4, 4)),
            dma((31,)), dma((31,)),
            dma((6, 4)), dma((6, 4)),
            dma((7,)), dma((7,)),
            dma((8,)),
        ],
        compiler_params=pltpu.CompilerParams(
            collective_id=0, has_side_effects=True, vmem_limit_bytes=54 * 1024 * 1024
        ),
        name="ffn_backward",
    )(out_grad.T, inputs.T, preact, up_weight, down_weight)
    return input_grad.T, up_grad, down_grad


def solution(mesh):
    placed = (
        P("wa", ("ia", "ao")),
        P("wa", ("ia", "ao")),
        P("wa", "ao"),
        P("ia", ("ao", "wa")),
        P(("ao", "wa"), "ia"),
    )
    return jax.shard_map(
        per_device,
        mesh=mesh,
        in_specs=placed,
        out_specs=(P("wa", ("ia", "ao")), P("ia", ("ao", "wa")), P(("ao", "wa"), "ia")),
        check_vma=False,
    )
```

```python
import jax
import jax.numpy as jnp
from jax import lax
from jax.experimental import pallas as pl
from jax.experimental.pallas import tpu as pltpu
from jax.sharding import PartitionSpec as P

MESH = pl.DeviceIdType.MESH
BF = jnp.bfloat16
F32 = jnp.float32
TOK = 320
FEAT = 192
BLK = 480
DI = 1536
HI = 768
NT = (((1,), (1,)), ((), ()))
TN = (((0,), (0,)), ((), ()))
FWD = (0, 3)

ORDER = (
    ("grad", 0, 0, 0), ("grad",), ("grad", 0, 3, 0), ("tok",), ("activate", 0), ("grad", 0, 1, 0),
    ("grad", 1, 0, 0), ("grad", 0, 0, 3), ("grad", 0, 1, 1), ("grad", 1, 0, 3), ("grad", 1, 1, 0),
    ("grad", 1, 3, 0), ("grad", 0, 0, 1), ("grad", 0, 3, 3), ("grad", 0, 1, 3), ("grad", 0, 2, 0),
    ("grad", 1, 2, 0), ("grad", 1, 0, 1), ("grad", 1, 1, 1), ("grad", 0, 0, 2), ("grad", 1, 0, 2), ("f1", 0),
    ("grad", 1, 3, 3), ("tok", 1, 0, 0), ("grad", 1, 3, 1), ("grad", 0, 3, 2), ("grad", 0, 2, 3),
    ("grad", 0, 2, 1), ("f2", 0), ("grad", 1, 2, 1), ("grad", 0, 1, 2), ("grad", 0, 3, 1), ("grad", 1, 1, 3),
    ("grad", 1, 1, 2), ("f1", 1), ("grad", 1, 3, 2), ("grad", 1, 2, 3), ("pre_send",), ("f1", 3), ("f3", 0),
    ("f2", 1), ("grad", 1, 2, 2), ("grad", 0, 2, 2), ("tok", 1, 0, 1), ("tok", 1, 1, 0), ("f1", 2), ("f2", 3),
    ("f2", 2), ("f3", 1), ("f4", 0), ("tok", 0, 0, 0), ("pre_relay",), ("f3", 2), ("pre_get", 1),
    ("tok", 1, 0, 3), ("tok", 1, 3, 0), ("f4", 1), ("tok", 1, 2, 0), ("pre_get", 3), ("tok", 0, 3, 0),
    ("tok", 0, 0, 1), ("f5", 0), ("tok", 0, 1, 0), ("pre_get", 2), ("tok", 1, 1, 1), ("f4", 2), ("f5", 1),
    ("f6", 0), ("f3", 3), ("tok", 0, 0, 3), ("tok", 1, 1, 3), ("activate", 2), ("tok", 1, 3, 3), ("activate", 1),
    ("f5", 2), ("tok", 0, 2, 0), ("f6", 1), ("activate", 3), ("tok", 0, 1, 1), ("tok", 1, 2, 1), ("tok", 0, 3, 3),
    ("f4", 3), ("f7", 0), ("tok", 0, 2, 1),
    ("scatter",
     (),
     (("near", 1, 0), ("far", 0, 0),)),
    ("f6", 2), ("f7", 1), ("tok", 0, 3, 1),
    ("scatter",
     (),
     (("far", 1, 1), ("near", 1, 1),)),
    ("f5", 3), ("tok", 1, 2, 2), ("tok", 1, 0, 2), ("f7", 2),
    ("scatter",
     (),
     (("far", 0, 2),)),
    ("tok", 1, 1, 2),
    ("scatter",
     (),
     (("far", 1, 2),)),
    ("tok", 0, 2, 2),
    ("scatter",
     (("far", 0, 1),),
     (("near", 0, 2),)),
    ("down", 0, 1),
    ("scatter",
     (("far", 1, 3),),
     ()),
    ("tok", 0, 1, 3),
    ("scatter",
     (("far", 1, 2),),
     ()),
    ("tok", 1, 3, 2),
    ("scatter",
     (("far", 1, 1),),
     ()),
    ("tok", 1, 2, 3),
    ("scatter",
     (),
     (("near", 0, 1),)),
    ("f6", 3),
    ("scatter",
     (("near", 1, 2), ("far", 0, 0),),
     ()),
    ("down", 1, 2),
    ("scatter",
     (("near", 1, 1), ("far", 1, 0),),
     (("mid", 1, 1),)),
    ("tok", 0, 1, 2),
    ("scatter",
     (("far", 0, 2),),
     (("near", 1, 2), ("far", 0, 1),)),
    ("f7", 3),
    ("scatter",
     (("mid", 1, 2),),
     (("far", 1, 3), ("mid", 1, 2),)),
    ("tok", 0, 3, 2), ("down", 2, 3),
    ("scatter",
     (("mid", 1, 1), ("mid", 1, 3), ("near", 0, 2), ("mid", 0, 2),),
     (("near", 1, 3), ("far", 1, 0),)),
    ("down", 3, 4),
    ("scatter",
     (("near", 1, 3),),
     (("mid", 0, 2), ("mid", 1, 3), ("near", 0, 3), ("end", 1, 2), ("p_open", 1, 2), ("far", 0, 3),)),
    ("tok", 0, 2, 3),
    ("scatter",
     (),
     (("mid", 1, 0),)),
    ("tok", 1, 3, 1), ("down", 4, 5),
    ("scatter",
     (("near", 1, 0), ("far", 0, 3), ("mid", 1, 0),),
     ()),
    ("tok", 0, 0, 2),
    ("scatter",
     (("end", 1, 2), ("p_open", 1, 2),),
     (("end", 1, 1),)),
    ("unpack", 0), ("unpack", 1),
    ("scatter",
     (("end", 1, 1), ("mid", 0, 0),),
     (("end", 0, 2), ("mid", 0, 1), ("p_open", 1, 1), ("near", 0, 0), ("mid", 0, 0), ("p_open", 0, 2), ("end", 1, 3), ("p_mid", 1), ("mid", 0, 3),)),
    ("unpack", 3),
    ("scatter",
     (("p_open", 1, 1), ("near", 0, 0),),
     ()),
    ("unpack", 2),
    ("scatter",
     (("mid", 0, 1), ("end", 1, 3), ("end", 0, 2), ("near", 0, 1),),
     ()),
    ("upg", 0, 1),
    ("scatter",
     (("p_open", 0, 2), ("near", 0, 3), ("p_mid", 1),),
     ()),
    ("upg", 1, 3),
    ("scatter",
     (("mid", 0, 3), ("end", 1, 0), ("p_end", 1), ("end", 0, 1), ("end", 0, 3), ("p_mid", 0), ("p_open", 0, 3),),
     (("end", 1, 0), ("p_end", 1), ("end", 0, 1), ("p_mid", 0), ("end", 0, 3),)),
    ("upg", 3, 4), ("down", 5, 6),
    ("scatter",
     (("end", 0, 0),),
     (("p_open", 0, 3), ("end", 0, 0),)),
    ("upg", 4, 6),
    ("scatter",
     (("p_end", 0),),
     (("p_end", 0),)),
)


def gelu(u):
    square = u * u
    t = jnp.tanh(0.7978845608 * (u + 0.044715 * u * square))
    return 0.5 * u * (1.0 + t)


def slope(u):
    square = u * u
    t = jnp.tanh(0.7978845608 * (u + 0.044715 * u * square))
    return 0.5 * (1.0 + t) + 0.5 * u * (1.0 - t * t) * 0.7978845608 * (1.0 + 0.134145 * square)


def swap_halves(v):
    return pltpu.roll(v, 64, 1)


def low_lanes(shape):
    return lax.broadcasted_iota(jnp.int32, shape, 1) < 64


def loop(n, body):
    def step(i, carry):
        body(i)
        return carry

    lax.fori_loop(0, n, step, 0)


def kernel(
    grad_in, tok_in, preact, up_w, down_w,
    ig_out, ug, dg,
    cg, cx, ci, rs, g, xt, wd, wu, par, rc, r1, r2, s1, s2, pre, stage, act, hid,
    ag_send, ag_recv, rs_send, rs_recv, f_send, f_recv, p_send, p_recv, l_sem,
):
    ia, y, ao = lax.axis_index("ia"), lax.axis_index("wa"), lax.axis_index("ao")
    zl, c = ia // 2, ia % 2
    zh, x = ao // 4, ao % 4
    b0, b1 = zl % 2, zl // 2

    def dev(dx=0, dy=0, flip_zh=False, to_zl=None, flip_c=False):
        x_, y_ = (x + dx) % 4, (y + dy) % 4
        zh_ = 1 - zh if flip_zh else zh
        zl_ = zl if to_zl is None else to_zl
        c_ = 1 - c if flip_c else c
        return {"ia": zl_ * 2 + c_, "wa": y_, "ao": zh_ * 4 + x_}

    def dev_p(d):
        return dev(dx=d * (1 - c), dy=d * c)

    def dev_s(d):
        return dev(dx=d * c, dy=d * (1 - c))

    sibling = dev(flip_c=True)
    far_z = dev(flip_zh=True)
    zl1 = dev(to_zl=zl + 1 - 2 * b0)
    zl2 = dev(to_zl=zl + 2 - 4 * b1)

    sent = []

    def push(src, dst, ssem, rsem, to):
        copy = pltpu.make_async_remote_copy(
            src_ref=src, dst_ref=dst, send_sem=ssem, recv_sem=rsem, device_id=to, device_id_type=MESH
        )
        copy.start()
        sent.append(copy)

    def got(dst, rsem, frm):
        pltpu.make_async_remote_copy(
            src_ref=dst, dst_ref=dst, send_sem=l_sem.at[7], recv_sem=rsem, device_id=frm, device_id_type=MESH
        ).wait_recv()

    copies = [
        pltpu.make_async_copy(down_w, wd, l_sem.at[0]),
        pltpu.make_async_copy(up_w, wu, l_sem.at[1]),
        pltpu.make_async_copy(
            preact.at[:, pl.ds(pl.multiple_of(y * HI, 128), HI)], pre.at[0], l_sem.at[2]
        ),
    ]
    for copy in copies:
        copy.start()
    waiting = {0, 1, 2}

    def loaded(n):
        if n in waiting:
            waiting.remove(n)
            copies[n].wait()

    def slot(w, j, k, jr=None, kr=None):
        jr, kr = (j if jr is None else jr), (k if kr is None else kr)
        dx, dy = j + (k - j) * c, kr + (jr - kr) * c
        zh_ = 1 - zh if w else zh
        return dy * 8 + zh_ * 4 + (x + dx) % 4

    def pack(src, dst):
        own = slot(0, 0, 0)

        def place(main, mini, first, second):
            dst[own, 0:TOK, :] = src[main:main + 128, :].astype(F32).T.astype(BF)
            m = src[mini:mini + 64, :].astype(F32).T
            halves = (m[0:160], m[160:320])
            dst[own, TOK:BLK, :] = jnp.concatenate([halves[first], halves[second]], axis=1).astype(BF)

        @pl.when(x % 2 == 0)
        def _():
            place(0, 128, 0, 1)

        @pl.when(x % 2 == 1)
        def _():
            place(64, 0, 1, 0)

    def unpack(src, dst, r):
        def body(n):
            e = src.at[r * 8 + 2 * n]
            o = src.at[r * 8 + 2 * n + 1]
            rows = pl.ds(r * TOK, TOK)
            base = n * 384
            dst[rows, pl.ds(pl.multiple_of(base, 128), 128)] = e[0:TOK, :]
            dst[rows, pl.ds(pl.multiple_of(base + 256, 128), 128)] = o[0:TOK, :]
            p, q = e[TOK:BLK, :].astype(F32), o[TOK:BLK, :].astype(F32)
            low = low_lanes((160, 128))
            mid = pl.ds(pl.multiple_of(base + 128, 128), 128)
            dst[pl.ds(r * TOK, 160), mid] = jnp.where(low, p, q).astype(BF)
            dst[pl.ds(r * TOK + 160, 160), mid] = swap_halves(jnp.where(low, q, p)).astype(BF)

        loop(4, body)

    pack(grad_in, cg)
    pack(tok_in, cx)

    barrier = pltpu.get_barrier_semaphore()
    partners = [dev_p(1), dev_p(3), dev_s(1), dev_s(3), dev(dy=2), sibling, far_z, zl1, zl2]
    for partner in partners[0:4] + partners[5:]:
        pl.semaphore_signal(barrier, inc=1, device_id=partner, device_id_type=MESH)
    pl.semaphore_wait(barrier, 8)

    class Gather:
        def __init__(self, index, buf):
            self.index, self.buf, self.n, self.have = index, buf, 0, {(0, 0, 0)}

        def _push(self, w, j, k, jr, kr, to, wr=None):
            push(
                self.buf.at[slot(w, j, k)],
                self.buf.at[slot(w, j, k, jr, kr)],
                ag_send.at[self.index, self.n],
                ag_recv.at[self.index, w if wr is None else wr, jr, kr],
                to,
            )
            self.n += 1

        def p(self, w, j, d):
            self._push(w, j, 0, (j - d) % 4, 0, dev_p(d))

        def s(self, w, j, k, d):
            self._push(w, j, k, j, (k - d) % 4, dev_s(d))

        def far(self):
            self._push(0, 0, 0, 0, 0, far_z, wr=1)

        def get(self, w, j, k):
            if (w, j, k) in self.have:
                return
            self.have.add((w, j, k))
            got(self.buf.at[slot(w, j, k)], ag_recv.at[self.index, w, j, k], dev_p(1))
            if k == 0:
                if j == 0:
                    self.start(w)
                    return
                if w == 0 and j == 3:
                    self.p(w, j, 1)
                if w == 1 and j == 1:
                    self.p(w, j, 3)
                self.s(w, j, k, 1)
                self.s(w, j, k, 3)
            elif k == 3 and j in FWD:
                self.s(w, j, k, 1)
            elif k == 1 and j not in FWD:
                self.s(w, j, k, 3)

        def start(self, w):
            for d in (1, 3):
                self.p(w, 0, d)
                self.s(w, 0, 0, d)

        def tokens(self, r):
            for w in (0, 1):
                for i in (0, 1, 3, 2):
                    self.get(w, i, r)
                for i in (0, 1, 3, 2):
                    self.get(w, r, i)

    grad, tok = Gather(0, cg), Gather(1, cx)

    half = pl.ds(pl.multiple_of(c * 160, 16), 160)
    other = pl.ds(pl.multiple_of((1 - c) * 160, 16), 160)
    up = 1 + 2 * c

    def preact_send():
        def cols(d):
            return pl.ds(pl.multiple_of(((y + d) % 4) * HI, 128), HI)

        push(preact.at[half, cols(2)], stage, p_send.at[0], p_recv.at[0], dev(dy=up))
        for d in (1, 3):
            push(preact.at[half, cols(d)], pre.at[4 - d, half], p_send.at[d], p_recv.at[4 - d], dev(dy=d))

    def preact_relay():
        got(stage, p_recv.at[0], dev(dy=1))
        push(stage, pre.at[2, half], p_send.at[2], p_recv.at[2], dev(dy=up))

    def preact_get(r):
        got(pre.at[r, half], p_recv.at[r], dev(dy=1))
        push(pre.at[r, half], pre.at[r, half], p_send.at[3 + r], p_recv.at[3 + r], sibling)

    def activate(r):
        if r > 0:
            got(pre.at[r, other], p_recv.at[3 + r], sibling)
        else:
            loaded(2)

        def body(i):
            rows = pl.multiple_of(i * 32, 32)
            u = pre[r, pl.ds(rows, 32), :].astype(F32)
            act[pl.ds(r * TOK + rows, 32), :] = gelu(u).astype(BF)

        loop(10, body)

    rows80 = pl.ds(pl.multiple_of(c * 160 + b0 * 80, 16), 80)
    keep80, give80 = pl.ds(pl.multiple_of(b0 * 80, 16), 80), pl.ds(pl.multiple_of((1 - b0) * 80, 16), 80)
    peer80 = pl.ds(pl.multiple_of(c * 160 + (1 - b0) * 80, 16), 80)
    keep384 = pl.ds(pl.multiple_of(b1 * 384, 128), 384)
    give384 = pl.ds(pl.multiple_of((1 - b1) * 384, 128), 384)

    def f1(r):
        grad.tokens(r)
        unpack(cg, g, r)
        loaded(0)

        def body(n):
            cols = pl.ds(pl.multiple_of(n * 256, 256), 256)
            par[r, :, cols] = lax.dot_general(
                g[r * TOK:(r + 1) * TOK, :], wd[cols, :], NT, preferred_element_type=F32
            ).astype(BF)

        loop(3, body)
        push(par.at[r, other], rc.at[r], f_send.at[0, r], f_recv.at[0, r], sibling)

    def f2(r):
        got(rc.at[r], f_recv.at[0, r], sibling)
        s1[r] = (par[r, half, :].astype(F32) + rc[r].astype(F32)).astype(BF)
        push(s1.at[r, give80], r1.at[r], f_send.at[1, r], f_recv.at[1, r], zl1)

    def f3(r):
        got(r1.at[r], f_recv.at[1, r], zl1)
        s2[r] = (s1[r, keep80, :].astype(F32) + r1[r].astype(F32)).astype(BF)
        push(s2.at[r, :, give384], r2.at[r], f_send.at[2, r], f_recv.at[2, r], zl2)

    def hrows(r, ds):
        return pl.ds(pl.multiple_of(r * TOK + ds.start, 16), ds.size)

    def f4(r):
        if r == 0:
            loaded(2)
        got(r2.at[r], f_recv.at[2, r], zl2)
        total = s2[r, :, keep384].astype(F32) + r2[r].astype(F32)
        u = pre[r, rows80, keep384].astype(F32)
        hid[hrows(r, rows80), keep384] = (total * slope(u)).astype(BF)
        piece = hid.at[hrows(r, rows80), keep384]
        push(piece, piece, f_send.at[3, r], f_recv.at[3, r], zl2)

    def f5(r):
        got(hid.at[hrows(r, rows80), give384], f_recv.at[3, r], zl2)
        piece = hid.at[hrows(r, rows80), :]
        push(piece, piece, f_send.at[4, r], f_recv.at[4, r], zl1)

    def f6(r):
        got(hid.at[hrows(r, peer80), :], f_recv.at[4, r], zl1)
        piece = hid.at[hrows(r, half), :]
        push(piece, piece, f_send.at[5, r], f_recv.at[5, r], sibling)

    def f7(r):
        got(hid.at[hrows(r, other), :], f_recv.at[5, r], sibling)
        loaded(1)

        def body(n):
            cols = pl.ds(pl.multiple_of(n * 384, 128), 384)
            term = lax.dot_general(
                hid[r * TOK:(r + 1) * TOK, :], wu[cols, :], NT, preferred_element_type=F32
            )
            even, odd = r * 8 + 2 * n, r * 8 + 2 * n + 1
            ci[even, 0:TOK, :] = term[:, 0:128].astype(BF)
            ci[odd, 0:TOK, :] = term[:, 256:384].astype(BF)
            top, bot = term[0:160, 128:256], swap_halves(term[160:320, 128:256])
            low = low_lanes((160, 128))
            ci[even, TOK:BLK, :] = jnp.where(low, top, bot).astype(BF)
            ci[odd, TOK:BLK, :] = jnp.where(low, bot, top).astype(BF)

        loop(4, body)

    def down(lo, hi):
        def body(i):
            cols = pl.ds(pl.multiple_of((lo + i) * 256, 256), 256)
            dg[:, cols] = lax.dot_general(act[...], g[:, cols], TN, preferred_element_type=F32).astype(BF)

        loop(hi - lo, body)

    def upg(lo, hi):
        def body(i):
            cols = pl.ds(pl.multiple_of((lo + i) * 256, 256), 256)
            ug[cols, :] = lax.dot_general(xt[:, cols], hid[...], TN, preferred_element_type=F32).astype(BF)

        loop(hi - lo, body)

    def rs_push(block, index, to):
        pltpu.make_async_remote_copy(
            src_ref=ci.at[block], dst_ref=rs.at[index], send_sem=rs_send.at[index], recv_sem=rs_recv.at[index],
            device_id=to, device_id_type=MESH,
        ).start()

    def rs_add(block, *indices):
        total = ci[block].astype(F32)
        for index in indices:
            got(rs.at[index], rs_recv.at[index], dev_p(1))
            total = total + rs[index].astype(F32)
        return total

    def s_far(w, j):
        rs_push(slot(w, j, 2), (w * 4 + j) * 3, dev_s(1 if j in FWD else 3))

    def s_near(w, j):
        d = 3 if j in FWD else 1
        rs_push(slot(w, j, d), (w * 4 + j) * 3 + 2, dev_s(d))

    def s_mid(w, j):
        d, base = (1 if j in FWD else 3), (w * 4 + j) * 3
        block = slot(w, j, d)
        ci[block] = rs_add(block, base).astype(BF)
        rs_push(block, base + 1, dev_s(d))

    def s_end(w, j):
        base = (w * 4 + j) * 3
        block = slot(w, j, 0)
        ci[block] = rs_add(block, base + 1, base + 2).astype(BF)

    def p_open(w, j):
        d, base = (3 if w else 1), 24 + w * 3
        rs_push(slot(w, j, 0), base + (0 if j == 2 else 2), dev_p(d if j == 2 else 4 - d))

    def p_mid(w):
        d, base = (3 if w else 1), 24 + w * 3
        block = slot(w, d, 0)
        ci[block] = rs_add(block, base).astype(BF)
        rs_push(block, base + 1, dev_p(d))

    def p_end(w):
        base = 24 + w * 3
        block = slot(w, 0, 0)
        ci[block] = rs_add(block, base + 1, base + 2).astype(BF)
        if w:
            rs_push(block, 30, far_z)

    gathers = {"grad": grad, "tok": tok}
    steps = {
        "pre_send": preact_send, "pre_relay": preact_relay, "pre_get": preact_get, "activate": activate,
        "f1": f1, "f2": f2, "f3": f3, "f4": f4, "f5": f5, "f6": f6, "f7": f7,
        "unpack": lambda r: unpack(cx, xt, r), "down": down, "upg": upg,
    }
    scatter = {
        "far": s_far, "near": s_near, "mid": s_mid, "end": s_end,
        "p_open": p_open, "p_mid": p_mid, "p_end": p_end,
    }

    def run(name, *args):
        if name in gathers:
            gather = gathers[name]
            if args == (0, 0, 0):
                gather.start(0)
            elif args:
                gather.get(*args)
            else:
                gather.far()
        else:
            steps[name](*args)

    def by_core(core, work):
        if work:
            @pl.when(c == core)
            def _():
                for name, *args in work:
                    scatter[name](*args)

    for item in ORDER:
        if item[0] == "scatter":
            by_core(0, item[1])
            by_core(1, item[2])
        else:
            run(*item)
    total = rs_add(slot(0, 0, 0), 30)
    main, left, right = total[0:TOK], total[TOK:BLK, 0:64], total[TOK:BLK, 64:128]

    @pl.when(x % 2 == 0)
    def _():
        ig_out[0:128, :] = main.T.astype(BF)
        ig_out[128:192, :] = jnp.concatenate([left, right], axis=0).T.astype(BF)

    @pl.when(x % 2 == 1)
    def _():
        ig_out[64:192, :] = main.T.astype(BF)
        ig_out[0:64, :] = jnp.concatenate([right, left], axis=0).T.astype(BF)

    for copy in sent:
        copy.wait_send()
    for index in range(31):
        pltpu.make_async_remote_copy(
            src_ref=ci.at[0], dst_ref=rs.at[index], send_sem=rs_send.at[index], recv_sem=rs_recv.at[index],
            device_id=far_z, device_id_type=MESH,
        ).wait_send()


def per_device(inputs, out_grad, preact, up_weight, down_weight):
    vmem = pl.BlockSpec(memory_space=pltpu.VMEM)
    hbm = pl.BlockSpec(memory_space=pltpu.HBM)
    blocks = pltpu.VMEM((32, BLK, 128), BF)
    dma = pltpu.SemaphoreType.DMA
    tokens = 4 * TOK
    input_grad, up_grad, down_grad = pl.pallas_call(
        kernel,
        out_shape=(
            jax.ShapeDtypeStruct((FEAT, TOK), BF),
            pltpu.VMEM((DI, HI), BF),
            pltpu.VMEM((HI, DI), BF),
        ),
        in_specs=[vmem, vmem, hbm, hbm, hbm],
        out_specs=(vmem, vmem, vmem),
        scratch_shapes=[
            blocks, blocks, blocks,
            pltpu.VMEM((31, BLK, 128), BF),
            pltpu.VMEM((tokens, DI), BF),
            pltpu.VMEM((tokens, DI), BF),
            pltpu.VMEM((HI, DI), BF),
            pltpu.VMEM((DI, HI), BF),
            pltpu.VMEM((4, TOK, HI), BF),
            pltpu.VMEM((4, 160, HI), BF),
            pltpu.VMEM((4, 80, HI), BF),
            pltpu.VMEM((4, 80, 384), BF),
            pltpu.VMEM((4, 160, HI), BF),
            pltpu.VMEM((4, 80, HI), BF),
            pltpu.VMEM((4, TOK, HI), BF),
            pltpu.VMEM((160, HI), BF),
            pltpu.VMEM((tokens, HI), BF),
            pltpu.VMEM((tokens, HI), BF),
            dma((2, 31)), dma((2, 2, 4, 4)),
            dma((31,)), dma((31,)),
            dma((6, 4)), dma((6, 4)),
            dma((7,)), dma((7,)),
            dma((8,)),
        ],
        compiler_params=pltpu.CompilerParams(
            collective_id=0, has_side_effects=True, vmem_limit_bytes=54 * 1024 * 1024
        ),
        name="ffn_backward",
    )(out_grad.T, inputs.T, preact, up_weight, down_weight)
    return input_grad.T, up_grad, down_grad


def solution(mesh):
    placed = (
        P("wa", ("ia", "ao")),
        P("wa", ("ia", "ao")),
        P("wa", "ao"),
        P("ia", ("ao", "wa")),
        P(("ao", "wa"), "ia"),
    )
    return jax.shard_map(
        per_device,
        mesh=mesh,
        in_specs=placed,
        out_specs=(P("wa", ("ia", "ao")), P("ia", ("ao", "wa")), P(("ao", "wa"), "ia")),
        check_vma=False,
    )
```

```python
import jax
import jax.numpy as jnp
from jax import lax
from jax.experimental import pallas as pl
from jax.experimental.pallas import tpu as pltpu
from jax.sharding import PartitionSpec as P

MESH = pl.DeviceIdType.MESH
BF = jnp.bfloat16
F32 = jnp.float32
TOK = 320
FEAT = 192
BLK = 480
DI = 1536
HI = 768
NT = (((1,), (1,)), ((), ()))
TN = (((0,), (0,)), ((), ()))
FWD = (0, 3)

ORDER = (
    ("grad", 0, 0, 0), ("grad",), ("grad", 0, 3, 0), ("grad", 0, 1, 0), ("grad", 1, 0, 0), ("tok",),
    ("grad", 0, 0, 3), ("grad", 0, 2, 0), ("grad", 1, 0, 3), ("grad", 1, 1, 0), ("grad", 1, 3, 0),
    ("grad", 0, 0, 2), ("grad", 0, 1, 1), ("activate", 0), ("grad", 0, 3, 1), ("grad", 0, 0, 1),
    ("grad", 1, 0, 1), ("grad", 0, 3, 3), ("grad", 1, 0, 2), ("grad", 1, 2, 0), ("grad", 1, 1, 1), ("f1", 0),
    ("grad", 1, 3, 3), ("grad", 0, 1, 2), ("grad", 0, 2, 1), ("grad", 1, 2, 1), ("pre_send",), ("grad", 1, 1, 3),
    ("f2", 0), ("grad", 0, 1, 3), ("grad", 1, 1, 2), ("grad", 1, 3, 1), ("f1", 1), ("grad", 0, 2, 2),
    ("grad", 0, 2, 3), ("grad", 0, 3, 2), ("tok", 1, 0, 0), ("grad", 1, 3, 2), ("grad", 1, 2, 3), ("f3", 0),
    ("f2", 1), ("grad", 1, 2, 2), ("f1", 2), ("pre_relay",), ("f4", 0), ("tok", 0, 0, 0), ("f2", 2), ("f3", 1),
    ("pre_get", 1), ("tok", 1, 1, 0), ("f5", 0), ("f1", 3), ("f3", 2), ("tok", 0, 3, 0), ("f4", 1),
    ("tok", 0, 1, 0), ("pre_get", 2), ("tok", 0, 0, 1), ("tok", 0, 0, 3), ("f2", 3), ("activate", 1), ("f6", 0),
    ("f4", 2), ("tok", 1, 2, 0), ("tok", 0, 2, 0), ("f5", 1), ("tok", 0, 3, 3), ("tok", 0, 1, 3),
    ("tok", 1, 3, 0), ("tok", 0, 1, 1), ("f3", 3), ("f7", 0), ("tok", 1, 0, 3), ("f5", 2), ("f6", 1),
    ("pre_get", 3), ("tok", 0, 2, 1), ("tok", 1, 2, 1),
    ("scatter",
     (),
     (("near", 1, 0), ("far", 0, 0),)),
    ("f4", 3), ("tok", 0, 2, 3), ("tok", 1, 3, 3), ("f7", 1), ("f6", 2),
    ("scatter",
     (("near", 1, 2),),
     (("far", 1, 0), ("far", 0, 1), ("far", 1, 1),)),
    ("tok", 1, 2, 3),
    ("scatter",
     (),
     (("near", 0, 1),)),
    ("f5", 3), ("tok", 1, 1, 1), ("tok", 0, 3, 2),
    ("scatter",
     (("near", 0, 2),),
     ()),
    ("tok", 1, 0, 2), ("activate", 3), ("f7", 2),
    ("scatter",
     (("far", 1, 3), ("far", 1, 1),),
     (("mid", 1, 0),)),
    ("f6", 3),
    ("scatter",
     (),
     (("near", 1, 1),)),
    ("activate", 2),
    ("scatter",
     (("far", 1, 2),),
     ()),
    ("tok", 0, 3, 1),
    ("scatter",
     (("far", 1, 0), ("far", 0, 0), ("far", 0, 1), ("far", 0, 3), ("near", 1, 1),),
     (("far", 1, 2),)),
    ("tok", 1, 3, 1), ("tok", 0, 0, 2),
    ("scatter",
     (("far", 0, 2),),
     (("mid", 1, 1), ("mid", 0, 0),)),
    ("tok", 1, 1, 2), ("f7", 3),
    ("scatter",
     (("mid", 1, 2),),
     (("far", 1, 3), ("near", 1, 3), ("near", 1, 2), ("mid", 1, 2),)),
    ("down", 0, 1),
    ("scatter",
     (("mid", 1, 1), ("near", 0, 3),),
     (("far", 0, 3), ("end", 1, 0),)),
    ("down", 1, 2),
    ("scatter",
     (("mid", 1, 3), ("mid", 0, 0),),
     (("far", 0, 2), ("end", 1, 1),)),
    ("tok", 1, 1, 3),
    ("scatter",
     (("near", 1, 3),),
     ()),
    ("down", 2, 3),
    ("scatter",
     (("end", 1, 2), ("p_open", 1, 2), ("mid", 0, 2),),
     (("mid", 1, 3),)),
    ("down", 3, 4),
    ("scatter",
     (),
     (("end", 1, 2),)),
    ("tok", 1, 3, 2),
    ("scatter",
     (("mid", 1, 0), ("end", 1, 1), ("p_open", 1, 1), ("near", 1, 0),),
     (("p_open", 1, 2),)),
    ("down", 4, 5), ("tok", 1, 0, 1),
    ("scatter",
     (("mid", 0, 3), ("end", 1, 3), ("p_mid", 1), ("near", 0, 0),),
     (("near", 0, 2), ("mid", 0, 2),)),
    ("unpack", 0),
    ("scatter",
     (),
     (("p_open", 1, 1),)),
    ("tok", 0, 1, 2),
    ("scatter",
     (),
     (("mid", 0, 3),)),
    ("unpack", 3),
    ("scatter",
     (),
     (("end", 1, 3), ("mid", 0, 1), ("p_mid", 1),)),
    ("tok", 1, 2, 2), ("tok", 0, 2, 2),
    ("scatter",
     (("end", 0, 2),),
     ()),
    ("unpack", 2),
    ("scatter",
     (("near", 0, 1), ("mid", 0, 1),),
     (("near", 0, 3),)),
    ("unpack", 1),
    ("scatter",
     (("p_open", 0, 2), ("end", 1, 0), ("p_end", 1),),
     (("near", 0, 0), ("end", 0, 2), ("p_open", 0, 2),)),
    ("upg", 0, 2),
    ("scatter",
     (),
     (("p_end", 1),)),
    ("upg", 2, 3),
    ("scatter",
     (("end", 0, 3), ("p_open", 0, 3), ("end", 0, 1), ("p_mid", 0), ("end", 0, 0),),
     (("end", 0, 1), ("p_mid", 0), ("end", 0, 0), ("end", 0, 3), ("p_open", 0, 3),)),
    ("down", 5, 6), ("upg", 3, 6),
    ("scatter",
     (("p_end", 0),),
     (("p_end", 0),)),
)


def gelu(u):
    square = u * u
    t = jnp.tanh(0.7978845608 * (u + 0.044715 * u * square))
    return 0.5 * u * (1.0 + t)


def slope(u):
    square = u * u
    t = jnp.tanh(0.7978845608 * (u + 0.044715 * u * square))
    return 0.5 * (1.0 + t) + 0.5 * u * (1.0 - t * t) * 0.7978845608 * (1.0 + 0.134145 * square)


def swap_halves(v):
    return pltpu.roll(v, 64, 1)


def low_lanes(shape):
    return lax.broadcasted_iota(jnp.int32, shape, 1) < 64


def loop(n, body):
    def step(i, carry):
        body(i)
        return carry

    lax.fori_loop(0, n, step, 0)


def kernel(
    grad_in, tok_in, preact, up_w, down_w,
    ig_out, ug, dg,
    cg, cx, ci, rs, g, xt, wd, wu, par, rc, r1, r2, s1, s2, pre, stage, act, hid,
    ag_send, ag_recv, rs_send, rs_recv, f_send, f_recv, p_send, p_recv, l_sem,
):
    ia, y, ao = lax.axis_index("ia"), lax.axis_index("wa"), lax.axis_index("ao")
    zl, c = ia // 2, ia % 2
    zh, x = ao // 4, ao % 4
    b0, b1 = zl % 2, zl // 2

    def dev(dx=0, dy=0, flip_zh=False, to_zl=None, flip_c=False):
        x_, y_ = (x + dx) % 4, (y + dy) % 4
        zh_ = 1 - zh if flip_zh else zh
        zl_ = zl if to_zl is None else to_zl
        c_ = 1 - c if flip_c else c
        return {"ia": zl_ * 2 + c_, "wa": y_, "ao": zh_ * 4 + x_}

    def dev_p(d):
        return dev(dx=d * (1 - c), dy=d * c)

    def dev_s(d):
        return dev(dx=d * c, dy=d * (1 - c))

    sibling = dev(flip_c=True)
    far_z = dev(flip_zh=True)
    zl1 = dev(to_zl=zl + 1 - 2 * b0)
    zl2 = dev(to_zl=zl + 2 - 4 * b1)

    sent = []

    def push(src, dst, ssem, rsem, to):
        copy = pltpu.make_async_remote_copy(
            src_ref=src, dst_ref=dst, send_sem=ssem, recv_sem=rsem, device_id=to, device_id_type=MESH
        )
        copy.start()
        sent.append(copy)

    def got(dst, rsem, frm):
        pltpu.make_async_remote_copy(
            src_ref=dst, dst_ref=dst, send_sem=l_sem.at[7], recv_sem=rsem, device_id=frm, device_id_type=MESH
        ).wait_recv()

    copies = [
        pltpu.make_async_copy(down_w, wd, l_sem.at[0]),
        pltpu.make_async_copy(up_w, wu, l_sem.at[1]),
        pltpu.make_async_copy(
            preact.at[:, pl.ds(pl.multiple_of(y * HI, 128), HI)], pre.at[0], l_sem.at[2]
        ),
    ]
    for copy in copies:
        copy.start()
    waiting = {0, 1, 2}

    def loaded(n):
        if n in waiting:
            waiting.remove(n)
            copies[n].wait()

    def slot(w, j, k, jr=None, kr=None):
        jr, kr = (j if jr is None else jr), (k if kr is None else kr)
        dx, dy = j + (k - j) * c, kr + (jr - kr) * c
        zh_ = 1 - zh if w else zh
        return dy * 8 + zh_ * 4 + (x + dx) % 4

    def pack(src, dst):
        own = slot(0, 0, 0)

        def place(main, mini, first, second):
            dst[own, 0:TOK, :] = src[main:main + 128, :].astype(F32).T.astype(BF)
            m = src[mini:mini + 64, :].astype(F32).T
            halves = (m[0:160], m[160:320])
            dst[own, TOK:BLK, :] = jnp.concatenate([halves[first], halves[second]], axis=1).astype(BF)

        @pl.when(x % 2 == 0)
        def _():
            place(0, 128, 0, 1)

        @pl.when(x % 2 == 1)
        def _():
            place(64, 0, 1, 0)

    def unpack(src, dst, r):
        def body(n):
            e = src.at[r * 8 + 2 * n]
            o = src.at[r * 8 + 2 * n + 1]
            rows = pl.ds(r * TOK, TOK)
            base = n * 384
            dst[rows, pl.ds(pl.multiple_of(base, 128), 128)] = e[0:TOK, :]
            dst[rows, pl.ds(pl.multiple_of(base + 256, 128), 128)] = o[0:TOK, :]
            p, q = e[TOK:BLK, :].astype(F32), o[TOK:BLK, :].astype(F32)
            low = low_lanes((160, 128))
            mid = pl.ds(pl.multiple_of(base + 128, 128), 128)
            dst[pl.ds(r * TOK, 160), mid] = jnp.where(low, p, q).astype(BF)
            dst[pl.ds(r * TOK + 160, 160), mid] = swap_halves(jnp.where(low, q, p)).astype(BF)

        loop(4, body)

    pack(grad_in, cg)

    barrier = pltpu.get_barrier_semaphore()
    partners = [dev_p(1), dev_p(3), dev_s(1), dev_s(3), dev(dy=2), sibling, far_z, zl1, zl2]
    for partner in partners[0:4] + partners[5:]:
        pl.semaphore_signal(barrier, inc=1, device_id=partner, device_id_type=MESH)
    pl.semaphore_wait(barrier, 8)

    class Gather:
        def __init__(self, index, buf):
            self.index, self.buf, self.n, self.have = index, buf, 0, {(0, 0, 0)}

        def _push(self, w, j, k, jr, kr, to, wr=None):
            push(
                self.buf.at[slot(w, j, k)],
                self.buf.at[slot(w, j, k, jr, kr)],
                ag_send.at[self.index, self.n],
                ag_recv.at[self.index, w if wr is None else wr, jr, kr],
                to,
            )
            self.n += 1

        def p(self, w, j, d):
            self._push(w, j, 0, (j - d) % 4, 0, dev_p(d))

        def s(self, w, j, k, d):
            self._push(w, j, k, j, (k - d) % 4, dev_s(d))

        def far(self):
            self._push(0, 0, 0, 0, 0, far_z, wr=1)

        def get(self, w, j, k):
            if (w, j, k) in self.have:
                return
            self.have.add((w, j, k))
            got(self.buf.at[slot(w, j, k)], ag_recv.at[self.index, w, j, k], dev_p(1))
            if k == 0:
                if j == 0:
                    self.start(w)
                    return
                if w == 0 and j == 3:
                    self.p(w, j, 1)
                if w == 1 and j == 1:
                    self.p(w, j, 3)
                self.s(w, j, k, 1)
                self.s(w, j, k, 3)
            elif k == 3 and j in FWD:
                self.s(w, j, k, 1)
            elif k == 1 and j not in FWD:
                self.s(w, j, k, 3)

        def start(self, w):
            for d in (1, 3):
                self.p(w, 0, d)
                self.s(w, 0, 0, d)

        def tokens(self, r):
            for w in (0, 1):
                for i in (0, 1, 3, 2):
                    self.get(w, i, r)
                for i in (0, 1, 3, 2):
                    self.get(w, r, i)

    grad, tok = Gather(0, cg), Gather(1, cx)

    half = pl.ds(pl.multiple_of(c * 160, 16), 160)
    other = pl.ds(pl.multiple_of((1 - c) * 160, 16), 160)
    up = 1 + 2 * c

    def preact_send():
        def cols(d):
            return pl.ds(pl.multiple_of(((y + d) % 4) * HI, 128), HI)

        push(preact.at[half, cols(2)], stage, p_send.at[0], p_recv.at[0], dev(dy=up))
        for d in (1, 3):
            push(preact.at[half, cols(d)], pre.at[4 - d, half], p_send.at[d], p_recv.at[4 - d], dev(dy=d))

    def preact_relay():
        got(stage, p_recv.at[0], dev(dy=1))
        push(stage, pre.at[2, half], p_send.at[2], p_recv.at[2], dev(dy=up))

    def preact_get(r):
        got(pre.at[r, half], p_recv.at[r], dev(dy=1))
        push(pre.at[r, half], pre.at[r, half], p_send.at[3 + r], p_recv.at[3 + r], sibling)

    def activate(r):
        if r > 0:
            got(pre.at[r, other], p_recv.at[3 + r], sibling)
        else:
            loaded(2)

        def body(i):
            rows = pl.multiple_of(i * 32, 32)
            u = pre[r, pl.ds(rows, 32), :].astype(F32)
            act[pl.ds(r * TOK + rows, 32), :] = gelu(u).astype(BF)

        loop(10, body)

    rows80 = pl.ds(pl.multiple_of(c * 160 + b0 * 80, 16), 80)
    keep80, give80 = pl.ds(pl.multiple_of(b0 * 80, 16), 80), pl.ds(pl.multiple_of((1 - b0) * 80, 16), 80)
    peer80 = pl.ds(pl.multiple_of(c * 160 + (1 - b0) * 80, 16), 80)
    keep384 = pl.ds(pl.multiple_of(b1 * 384, 128), 384)
    give384 = pl.ds(pl.multiple_of((1 - b1) * 384, 128), 384)

    def f1(r):
        grad.tokens(r)
        unpack(cg, g, r)
        loaded(0)

        def body(n):
            cols = pl.ds(pl.multiple_of(n * 256, 256), 256)
            par[r, :, cols] = lax.dot_general(
                g[r * TOK:(r + 1) * TOK, :], wd[cols, :], NT, preferred_element_type=F32
            ).astype(BF)

        loop(3, body)
        push(par.at[r, other], rc.at[r], f_send.at[0, r], f_recv.at[0, r], sibling)

    def f2(r):
        got(rc.at[r], f_recv.at[0, r], sibling)
        s1[r] = (par[r, half, :].astype(F32) + rc[r].astype(F32)).astype(BF)
        push(s1.at[r, give80], r1.at[r], f_send.at[1, r], f_recv.at[1, r], zl1)

    def f3(r):
        got(r1.at[r], f_recv.at[1, r], zl1)
        s2[r] = (s1[r, keep80, :].astype(F32) + r1[r].astype(F32)).astype(BF)
        push(s2.at[r, :, give384], r2.at[r], f_send.at[2, r], f_recv.at[2, r], zl2)

    def hrows(r, ds):
        return pl.ds(pl.multiple_of(r * TOK + ds.start, 16), ds.size)

    def f4(r):
        if r == 0:
            loaded(2)
        got(r2.at[r], f_recv.at[2, r], zl2)
        total = s2[r, :, keep384].astype(F32) + r2[r].astype(F32)
        u = pre[r, rows80, keep384].astype(F32)
        hid[hrows(r, rows80), keep384] = (total * slope(u)).astype(BF)
        piece = hid.at[hrows(r, rows80), keep384]
        push(piece, piece, f_send.at[3, r], f_recv.at[3, r], zl2)

    def f5(r):
        got(hid.at[hrows(r, rows80), give384], f_recv.at[3, r], zl2)
        piece = hid.at[hrows(r, rows80), :]
        push(piece, piece, f_send.at[4, r], f_recv.at[4, r], zl1)

    def f6(r):
        got(hid.at[hrows(r, peer80), :], f_recv.at[4, r], zl1)
        piece = hid.at[hrows(r, half), :]
        push(piece, piece, f_send.at[5, r], f_recv.at[5, r], sibling)

    def f7(r):
        got(hid.at[hrows(r, other), :], f_recv.at[5, r], sibling)
        loaded(1)

        def body(n):
            cols = pl.ds(pl.multiple_of(n * 768, 256), 768)
            term = lax.dot_general(
                hid[r * TOK:(r + 1) * TOK, :], wu[cols, :], NT, preferred_element_type=F32
            )
            low = low_lanes((160, 128))
            for q in (0, 1):
                even, lane = r * 8 + 4 * n + 2 * q, q * 384
                ci[even, 0:TOK, :] = term[:, lane:lane + 128].astype(BF)
                ci[even + 1, 0:TOK, :] = term[:, lane + 256:lane + 384].astype(BF)
                mid = term[:, lane + 128:lane + 256]
                top, bot = mid[0:160], swap_halves(mid[160:320])
                ci[even, TOK:BLK, :] = jnp.where(low, top, bot).astype(BF)
                ci[even + 1, TOK:BLK, :] = jnp.where(low, bot, top).astype(BF)

        loop(2, body)

    def down(lo, hi):
        def body(i):
            cols = pl.ds(pl.multiple_of((lo + i) * 256, 256), 256)
            dg[:, cols] = lax.dot_general(act[...], g[:, cols], TN, preferred_element_type=F32).astype(BF)

        loop(hi - lo, body)

    def upg(lo, hi):
        def body(i):
            cols = pl.ds(pl.multiple_of((lo + i) * 256, 256), 256)
            ug[cols, :] = lax.dot_general(xt[:, cols], hid[...], TN, preferred_element_type=F32).astype(BF)

        loop(hi - lo, body)

    def rs_push(block, index, to):
        pltpu.make_async_remote_copy(
            src_ref=ci.at[block], dst_ref=rs.at[index], send_sem=rs_send.at[index], recv_sem=rs_recv.at[index],
            device_id=to, device_id_type=MESH,
        ).start()

    def rs_add(block, *indices):
        total = ci[block].astype(F32)
        for index in indices:
            got(rs.at[index], rs_recv.at[index], dev_p(1))
            total = total + rs[index].astype(F32)
        return total

    def s_far(w, j):
        rs_push(slot(w, j, 2), (w * 4 + j) * 3, dev_s(1 if j in FWD else 3))

    def s_near(w, j):
        d = 3 if j in FWD else 1
        rs_push(slot(w, j, d), (w * 4 + j) * 3 + 2, dev_s(d))

    def s_mid(w, j):
        d, base = (1 if j in FWD else 3), (w * 4 + j) * 3
        block = slot(w, j, d)
        ci[block] = rs_add(block, base).astype(BF)
        rs_push(block, base + 1, dev_s(d))

    def s_end(w, j):
        base = (w * 4 + j) * 3
        block = slot(w, j, 0)
        ci[block] = rs_add(block, base + 1, base + 2).astype(BF)

    def p_open(w, j):
        d, base = (3 if w else 1), 24 + w * 3
        rs_push(slot(w, j, 0), base + (0 if j == 2 else 2), dev_p(d if j == 2 else 4 - d))

    def p_mid(w):
        d, base = (3 if w else 1), 24 + w * 3
        block = slot(w, d, 0)
        ci[block] = rs_add(block, base).astype(BF)
        rs_push(block, base + 1, dev_p(d))

    def p_end(w):
        base = 24 + w * 3
        block = slot(w, 0, 0)
        ci[block] = rs_add(block, base + 1, base + 2).astype(BF)
        if w:
            rs_push(block, 30, far_z)

    gathers = {"grad": grad, "tok": tok}
    steps = {
        "pre_send": preact_send, "pre_relay": preact_relay, "pre_get": preact_get, "activate": activate,
        "f1": f1, "f2": f2, "f3": f3, "f4": f4, "f5": f5, "f6": f6, "f7": f7,
        "unpack": lambda r: unpack(cx, xt, r), "down": down, "upg": upg,
    }
    scatter = {
        "far": s_far, "near": s_near, "mid": s_mid, "end": s_end,
        "p_open": p_open, "p_mid": p_mid, "p_end": p_end,
    }

    def run(name, *args):
        if name in gathers:
            gather = gathers[name]
            if args == (0, 0, 0):
                gather.start(0)
            elif args:
                gather.get(*args)
            else:
                gather.far()
        else:
            steps[name](*args)

    def by_core(core, work):
        if work:
            @pl.when(c == core)
            def _():
                for name, *args in work:
                    scatter[name](*args)

    packed = False
    for item in ORDER:
        if item[0] == "tok" and not packed:
            pack(tok_in, cx)
            packed = True
        if item[0] == "scatter":
            by_core(0, item[1])
            by_core(1, item[2])
        else:
            run(*item)
    total = rs_add(slot(0, 0, 0), 30)
    main, left, right = total[0:TOK], total[TOK:BLK, 0:64], total[TOK:BLK, 64:128]

    @pl.when(x % 2 == 0)
    def _():
        ig_out[0:128, :] = main.T.astype(BF)
        ig_out[128:192, :] = jnp.concatenate([left, right], axis=0).T.astype(BF)

    @pl.when(x % 2 == 1)
    def _():
        ig_out[64:192, :] = main.T.astype(BF)
        ig_out[0:64, :] = jnp.concatenate([right, left], axis=0).T.astype(BF)

    for copy in sent:
        copy.wait_send()
    for index in range(31):
        pltpu.make_async_remote_copy(
            src_ref=ci.at[0], dst_ref=rs.at[index], send_sem=rs_send.at[index], recv_sem=rs_recv.at[index],
            device_id=far_z, device_id_type=MESH,
        ).wait_send()


def per_device(inputs, out_grad, preact, up_weight, down_weight):
    vmem = pl.BlockSpec(memory_space=pltpu.VMEM)
    hbm = pl.BlockSpec(memory_space=pltpu.HBM)
    blocks = pltpu.VMEM((32, BLK, 128), BF)
    dma = pltpu.SemaphoreType.DMA
    tokens = 4 * TOK
    input_grad, up_grad, down_grad = pl.pallas_call(
        kernel,
        out_shape=(
            jax.ShapeDtypeStruct((FEAT, TOK), BF),
            pltpu.VMEM((DI, HI), BF),
            pltpu.VMEM((HI, DI), BF),
        ),
        in_specs=[vmem, vmem, hbm, hbm, hbm],
        out_specs=(vmem, vmem, vmem),
        scratch_shapes=[
            blocks, blocks, blocks,
            pltpu.VMEM((31, BLK, 128), BF),
            pltpu.VMEM((tokens, DI), BF),
            pltpu.VMEM((tokens, DI), BF),
            pltpu.VMEM((HI, DI), BF),
            pltpu.VMEM((DI, HI), BF),
            pltpu.VMEM((4, TOK, HI), BF),
            pltpu.VMEM((4, 160, HI), BF),
            pltpu.VMEM((4, 80, HI), BF),
            pltpu.VMEM((4, 80, 384), BF),
            pltpu.VMEM((4, 160, HI), BF),
            pltpu.VMEM((4, 80, HI), BF),
            pltpu.VMEM((4, TOK, HI), BF),
            pltpu.VMEM((160, HI), BF),
            pltpu.VMEM((tokens, HI), BF),
            pltpu.VMEM((tokens, HI), BF),
            dma((2, 31)), dma((2, 2, 4, 4)),
            dma((31,)), dma((31,)),
            dma((6, 4)), dma((6, 4)),
            dma((7,)), dma((7,)),
            dma((8,)),
        ],
        compiler_params=pltpu.CompilerParams(
            collective_id=0, has_side_effects=True, vmem_limit_bytes=54 * 1024 * 1024
        ),
        name="ffn_backward",
    )(out_grad.T, inputs.T, preact, up_weight, down_weight)
    return input_grad.T, up_grad, down_grad


def solution(mesh):
    placed = (
        P("wa", ("ia", "ao")),
        P("wa", ("ia", "ao")),
        P("wa", "ao"),
        P("ia", ("ao", "wa")),
        P(("ao", "wa"), "ia"),
    )
    return jax.shard_map(
        per_device,
        mesh=mesh,
        in_specs=placed,
        out_specs=(P("wa", ("ia", "ao")), P("ia", ("ao", "wa")), P(("ao", "wa"), "ia")),
        check_vma=False,
    )
```

```python
import jax
import jax.numpy as jnp
from jax import lax
from jax.experimental import pallas as pl
from jax.experimental.pallas import tpu as pltpu
from jax.sharding import PartitionSpec as P

MESH = pl.DeviceIdType.MESH
BF = jnp.bfloat16
F32 = jnp.float32
TOK = 320
FEAT = 192
BLK = 480
DI = 1536
HI = 768
NT = (((1,), (1,)), ((), ()))
TN = (((0,), (0,)), ((), ()))
FWD = (0, 3)

ORDER = (
    ("grad",), ("grad", 0, 0, 0), ("tok", 0, 0, 0), ("grad", 0, 3, 0), ("grad", 0, 0, 1), ("grad", 0, 0, 3),
    ("grad", 1, 0, 0), ("grad", 0, 1, 0), ("grad", 1, 1, 0), ("grad", 1, 0, 3), ("grad", 0, 1, 1),
    ("grad", 1, 3, 0), ("tok",), ("grad", 0, 3, 3), ("grad", 0, 3, 1), ("grad", 1, 2, 0), ("grad", 0, 2, 0),
    ("grad", 1, 1, 1), ("grad", 0, 0, 2), ("activate", 0), ("grad", 1, 0, 2), ("grad", 1, 1, 3),
    ("grad", 1, 0, 1), ("f1", 0), ("grad", 0, 1, 3), ("grad", 1, 2, 1), ("grad", 1, 3, 3), ("grad", 0, 2, 1),
    ("grad", 0, 3, 2), ("pre_send",), ("tok", 0, 1, 0), ("f2", 0), ("grad", 0, 1, 2), ("grad", 1, 3, 1),
    ("grad", 1, 1, 2), ("f1", 1), ("grad", 1, 3, 2), ("grad", 1, 2, 2), ("grad", 0, 2, 3), ("grad", 1, 2, 3),
    ("grad", 0, 2, 2), ("f1", 2), ("f2", 1), ("tok", 1, 0, 0), ("f2", 2), ("f3", 0), ("f1", 3), ("f3", 1),
    ("pre_relay",), ("pre_get", 1), ("tok", 0, 0, 1), ("pre_get", 3), ("f3", 2), ("f2", 3), ("f4", 1),
    ("tok", 0, 3, 0), ("tok", 1, 1, 0), ("pre_get", 2), ("f4", 2), ("tok", 1, 3, 0), ("f3", 3), ("activate", 2),
    ("tok", 0, 3, 1), ("tok", 0, 2, 0), ("tok", 0, 1, 1), ("f5", 1), ("activate", 1), ("activate", 3),
    ("down", 0, 1), ("f5", 2), ("tok", 1, 2, 0), ("down", 1, 2), ("tok", 0, 0, 3), ("tok", 1, 0, 3), ("f4", 3),
    ("tok", 1, 0, 1), ("down", 2, 3), ("f6", 1), ("tok", 1, 3, 3), ("f4", 0), ("tok", 0, 3, 3), ("f6", 2),
    ("tok", 1, 1, 1), ("tok", 0, 2, 3), ("tok", 0, 2, 1), ("down", 3, 4), ("tok", 1, 2, 1), ("f5", 3), ("f7", 1),
    ("scatter",
     (),
     (("far", 1, 1),)),
    ("f5", 0), ("f7", 2),
    ("scatter",
     (("near", 1, 2), ("far", 1, 1), ("far", 1, 3),),
     ()),
    ("f6", 3),
    ("scatter",
     (("far", 1, 2), ("far", 0, 3), ("near", 1, 1), ("far", 0, 2),),
     (("near", 0, 1),)),
    ("tok", 0, 1, 2),
    ("scatter",
     (),
     (("near", 1, 2), ("far", 1, 2),)),
    ("tok", 0, 2, 2),
    ("scatter",
     (("far", 0, 1),),
     ()),
    ("tok", 0, 1, 3),
    ("scatter",
     (),
     (("near", 0, 2), ("mid", 1, 1), ("near", 1, 1),)),
    ("tok", 0, 0, 2),
    ("scatter",
     (),
     (("far", 0, 1), ("far", 0, 2),)),
    ("tok", 1, 0, 2),
    ("scatter",
     (("far", 1, 0),),
     ()),
    ("f6", 0), ("tok", 0, 3, 2), ("f7", 3),
    ("scatter",
     (("mid", 1, 2), ("near", 1, 0), ("far", 0, 0),),
     ()),
    ("tok", 1, 1, 2),
    ("scatter",
     (),
     (("far", 1, 3),)),
    ("tok", 1, 3, 1),
    ("scatter",
     (("mid", 1, 1), ("near", 0, 2),),
     (("mid", 1, 2),)),
    ("tok", 1, 1, 3),
    ("scatter",
     (("near", 1, 3), ("mid", 0, 2), ("mid", 1, 3),),
     (("near", 1, 3), ("far", 0, 3),)),
    ("f7", 0),
    ("scatter",
     (("end", 1, 2), ("p_open", 1, 2),),
     (("far", 1, 0), ("far", 0, 0),)),
    ("unpack", 0), ("tok", 1, 2, 2), ("tok", 1, 3, 2),
    ("scatter",
     (("mid", 0, 3),),
     ()),
    ("tok", 1, 2, 3),
    ("scatter",
     (("near", 0, 1),),
     ()),
    ("unpack", 3),
    ("scatter",
     (("mid", 1, 0), ("mid", 0, 0),),
     (("mid", 0, 2), ("end", 1, 2), ("mid", 1, 3), ("p_open", 1, 2),)),
    ("unpack", 2),
    ("scatter",
     (("end", 1, 1), ("p_open", 1, 1), ("near", 0, 3), ("end", 1, 3), ("p_mid", 1),),
     (("mid", 0, 1), ("mid", 1, 0), ("near", 1, 0), ("end", 1, 1), ("near", 0, 0),)),
    ("unpack", 1),
    ("scatter",
     (("end", 0, 2), ("mid", 0, 1), ("p_open", 0, 2),),
     (("p_open", 1, 1), ("mid", 0, 0), ("near", 0, 3), ("end", 0, 2), ("end", 1, 3), ("p_mid", 1), ("mid", 0, 3), ("end", 0, 1), ("p_open", 0, 2),)),
    ("down", 4, 5),
    ("scatter",
     (("near", 0, 0),),
     ()),
    ("upg", 0, 1),
    ("scatter",
     (("end", 0, 3), ("end", 1, 0), ("p_end", 1),),
     (("end", 1, 0),)),
    ("upg", 1, 2),
    ("scatter",
     (),
     (("p_end", 1),)),
    ("upg", 2, 3),
    ("scatter",
     (("end", 0, 1), ("p_mid", 0), ("p_open", 0, 3),),
     (("p_mid", 0), ("end", 0, 3), ("end", 0, 0), ("p_open", 0, 3),)),
    ("down", 5, 6), ("upg", 3, 4),
    ("scatter",
     (("end", 0, 0),),
     ()),
    ("upg", 4, 6),
    ("scatter",
     (("p_end", 0),),
     (("p_end", 0),)),
)


def gelu(u):
    square = u * u
    t = jnp.tanh(0.7978845608 * (u + 0.044715 * u * square))
    return 0.5 * u * (1.0 + t)


def slope(u):
    square = u * u
    t = jnp.tanh(0.7978845608 * (u + 0.044715 * u * square))
    return 0.5 * (1.0 + t) + 0.5 * u * (1.0 - t * t) * 0.7978845608 * (1.0 + 0.134145 * square)


def swap_halves(v):
    return pltpu.roll(v, 64, 1)


def low_lanes(shape):
    return lax.broadcasted_iota(jnp.int32, shape, 1) < 64


def loop(n, body):
    def step(i, carry):
        body(i)
        return carry

    lax.fori_loop(0, n, step, 0)


def kernel(
    grad_in, tok_in, preact, up_w, down_w,
    ig_out, ug, dg,
    cg, cx, ci, rs, g, xt, wd, wu, par, rc, r1, r2, s1, s2, pre, stage, act, hid,
    ag_send, ag_recv, rs_send, rs_recv, f_send, f_recv, p_send, p_recv, l_sem,
):
    ia, y, ao = lax.axis_index("ia"), lax.axis_index("wa"), lax.axis_index("ao")
    zl, c = ia // 2, ia % 2
    zh, x = ao // 4, ao % 4
    b0, b1 = zl % 2, zl // 2

    def dev(dx=0, dy=0, flip_zh=False, to_zl=None, flip_c=False):
        x_, y_ = (x + dx) % 4, (y + dy) % 4
        zh_ = 1 - zh if flip_zh else zh
        zl_ = zl if to_zl is None else to_zl
        c_ = 1 - c if flip_c else c
        return {"ia": zl_ * 2 + c_, "wa": y_, "ao": zh_ * 4 + x_}

    def dev_p(d):
        return dev(dx=d * (1 - c), dy=d * c)

    def dev_s(d):
        return dev(dx=d * c, dy=d * (1 - c))

    sibling = dev(flip_c=True)
    far_z = dev(flip_zh=True)
    zl1 = dev(to_zl=zl + 1 - 2 * b0)
    zl2 = dev(to_zl=zl + 2 - 4 * b1)

    sent = []

    def push(src, dst, ssem, rsem, to):
        copy = pltpu.make_async_remote_copy(
            src_ref=src, dst_ref=dst, send_sem=ssem, recv_sem=rsem, device_id=to, device_id_type=MESH
        )
        copy.start()
        sent.append(copy)

    def got(dst, rsem, frm):
        pltpu.make_async_remote_copy(
            src_ref=dst, dst_ref=dst, send_sem=l_sem.at[7], recv_sem=rsem, device_id=frm, device_id_type=MESH
        ).wait_recv()

    copies = [
        pltpu.make_async_copy(down_w, wd, l_sem.at[0]),
        pltpu.make_async_copy(up_w, wu, l_sem.at[1]),
        pltpu.make_async_copy(
            preact.at[:, pl.ds(pl.multiple_of(y * HI, 128), HI)], pre.at[0], l_sem.at[2]
        ),
    ]
    for copy in copies:
        copy.start()
    waiting = {0, 1, 2}

    def loaded(n):
        if n in waiting:
            waiting.remove(n)
            copies[n].wait()

    def slot(w, j, k, jr=None, kr=None):
        jr, kr = (j if jr is None else jr), (k if kr is None else kr)
        dx, dy = j + (k - j) * c, kr + (jr - kr) * c
        zh_ = 1 - zh if w else zh
        return dy * 8 + zh_ * 4 + (x + dx) % 4

    def pack(src, dst):
        own = slot(0, 0, 0)

        def place(main, mini, first, second):
            dst[own, 0:TOK, :] = src[main:main + 128, :].astype(F32).T.astype(BF)
            m = src[mini:mini + 64, :].astype(F32).T
            halves = (m[0:160], m[160:320])
            dst[own, TOK:BLK, :] = jnp.concatenate([halves[first], halves[second]], axis=1).astype(BF)

        @pl.when(x % 2 == 0)
        def _():
            place(0, 128, 0, 1)

        @pl.when(x % 2 == 1)
        def _():
            place(64, 0, 1, 0)

    def unpack(src, dst, r):
        def body(n):
            e = src.at[r * 8 + 2 * n]
            o = src.at[r * 8 + 2 * n + 1]
            rows = pl.ds(r * TOK, TOK)
            base = n * 384
            dst[rows, pl.ds(pl.multiple_of(base, 128), 128)] = e[0:TOK, :]
            dst[rows, pl.ds(pl.multiple_of(base + 256, 128), 128)] = o[0:TOK, :]
            p, q = e[TOK:BLK, :].astype(F32), o[TOK:BLK, :].astype(F32)
            low = low_lanes((160, 128))
            mid = pl.ds(pl.multiple_of(base + 128, 128), 128)
            dst[pl.ds(r * TOK, 160), mid] = jnp.where(low, p, q).astype(BF)
            dst[pl.ds(r * TOK + 160, 160), mid] = swap_halves(jnp.where(low, q, p)).astype(BF)

        loop(4, body)

    pack(grad_in, cg)

    barrier = pltpu.get_barrier_semaphore()
    partners = [dev_p(1), dev_p(3), dev_s(1), dev_s(3), dev(dy=2), sibling, far_z, zl1, zl2]
    for partner in partners[0:4] + partners[5:]:
        pl.semaphore_signal(barrier, inc=1, device_id=partner, device_id_type=MESH)
    pl.semaphore_wait(barrier, 8)

    class Gather:
        def __init__(self, index, buf):
            self.index, self.buf, self.n, self.have = index, buf, 0, {(0, 0, 0)}

        def _push(self, w, j, k, jr, kr, to, wr=None):
            push(
                self.buf.at[slot(w, j, k)],
                self.buf.at[slot(w, j, k, jr, kr)],
                ag_send.at[self.index, self.n],
                ag_recv.at[self.index, w if wr is None else wr, jr, kr],
                to,
            )
            self.n += 1

        def p(self, w, j, d):
            self._push(w, j, 0, (j - d) % 4, 0, dev_p(d))

        def s(self, w, j, k, d):
            self._push(w, j, k, j, (k - d) % 4, dev_s(d))

        def far(self):
            self._push(0, 0, 0, 0, 0, far_z, wr=1)

        def get(self, w, j, k):
            if (w, j, k) in self.have:
                return
            self.have.add((w, j, k))
            got(self.buf.at[slot(w, j, k)], ag_recv.at[self.index, w, j, k], dev_p(1))
            if k == 0:
                if j == 0:
                    self.start(w)
                    return
                if w == 0 and j == 3:
                    self.p(w, j, 1)
                if w == 1 and j == 1:
                    self.p(w, j, 3)
                self.s(w, j, k, 1)
                self.s(w, j, k, 3)
            elif k == 3 and j in FWD:
                self.s(w, j, k, 1)
            elif k == 1 and j not in FWD:
                self.s(w, j, k, 3)

        def start(self, w):
            for d in (1, 3):
                self.p(w, 0, d)
                self.s(w, 0, 0, d)

        def tokens(self, r):
            for w in (0, 1):
                for i in (0, 1, 3, 2):
                    self.get(w, i, r)
                for i in (0, 1, 3, 2):
                    self.get(w, r, i)

    grad, tok = Gather(0, cg), Gather(1, cx)

    half = pl.ds(pl.multiple_of(c * 160, 16), 160)
    other = pl.ds(pl.multiple_of((1 - c) * 160, 16), 160)
    up = 1 + 2 * c

    def preact_send():
        def cols(d):
            return pl.ds(pl.multiple_of(((y + d) % 4) * HI, 128), HI)

        push(preact.at[half, cols(2)], stage, p_send.at[0], p_recv.at[0], dev(dy=up))
        for d in (1, 3):
            push(preact.at[half, cols(d)], pre.at[4 - d, half], p_send.at[d], p_recv.at[4 - d], dev(dy=d))

    def preact_relay():
        got(stage, p_recv.at[0], dev(dy=1))
        push(stage, pre.at[2, half], p_send.at[2], p_recv.at[2], dev(dy=up))

    def preact_get(r):
        got(pre.at[r, half], p_recv.at[r], dev(dy=1))
        push(pre.at[r, half], pre.at[r, half], p_send.at[3 + r], p_recv.at[3 + r], sibling)

    def activate(r):
        if r > 0:
            got(pre.at[r, other], p_recv.at[3 + r], sibling)
        else:
            loaded(2)

        def body(i):
            rows = pl.multiple_of(i * 32, 32)
            u = pre[r, pl.ds(rows, 32), :].astype(F32)
            act[pl.ds(r * TOK + rows, 32), :] = gelu(u).astype(BF)

        loop(10, body)

    rows80 = pl.ds(pl.multiple_of(c * 160 + b0 * 80, 16), 80)
    keep80, give80 = pl.ds(pl.multiple_of(b0 * 80, 16), 80), pl.ds(pl.multiple_of((1 - b0) * 80, 16), 80)
    peer80 = pl.ds(pl.multiple_of(c * 160 + (1 - b0) * 80, 16), 80)
    keep384 = pl.ds(pl.multiple_of(b1 * 384, 128), 384)
    give384 = pl.ds(pl.multiple_of((1 - b1) * 384, 128), 384)

    def f1(r):
        grad.tokens(r)
        unpack(cg, g, r)
        loaded(0)

        def body(n):
            cols = pl.ds(pl.multiple_of(n * 256, 256), 256)
            par[r, :, cols] = lax.dot_general(
                g[r * TOK:(r + 1) * TOK, :], wd[cols, :], NT, preferred_element_type=F32
            ).astype(BF)

        loop(3, body)
        push(par.at[r, other], rc.at[r], f_send.at[0, r], f_recv.at[0, r], sibling)

    def f2(r):
        got(rc.at[r], f_recv.at[0, r], sibling)
        s1[r] = (par[r, half, :].astype(F32) + rc[r].astype(F32)).astype(BF)
        push(s1.at[r, give80], r1.at[r], f_send.at[1, r], f_recv.at[1, r], zl1)

    def f3(r):
        got(r1.at[r], f_recv.at[1, r], zl1)
        s2[r] = (s1[r, keep80, :].astype(F32) + r1[r].astype(F32)).astype(BF)
        push(s2.at[r, :, give384], r2.at[r], f_send.at[2, r], f_recv.at[2, r], zl2)

    def hrows(r, ds):
        return pl.ds(pl.multiple_of(r * TOK + ds.start, 16), ds.size)

    def f4(r):
        if r == 0:
            loaded(2)
        got(r2.at[r], f_recv.at[2, r], zl2)
        total = s2[r, :, keep384].astype(F32) + r2[r].astype(F32)
        u = pre[r, rows80, keep384].astype(F32)
        hid[hrows(r, rows80), keep384] = (total * slope(u)).astype(BF)
        piece = hid.at[hrows(r, rows80), keep384]
        push(piece, piece, f_send.at[3, r], f_recv.at[3, r], zl2)

    def f5(r):
        got(hid.at[hrows(r, rows80), give384], f_recv.at[3, r], zl2)
        piece = hid.at[hrows(r, rows80), :]
        push(piece, piece, f_send.at[4, r], f_recv.at[4, r], zl1)

    def f6(r):
        got(hid.at[hrows(r, peer80), :], f_recv.at[4, r], zl1)
        piece = hid.at[hrows(r, half), :]
        push(piece, piece, f_send.at[5, r], f_recv.at[5, r], sibling)

    def f7(r):
        got(hid.at[hrows(r, other), :], f_recv.at[5, r], sibling)
        loaded(1)

        def body(n):
            cols = pl.ds(pl.multiple_of(n * 768, 256), 768)
            term = lax.dot_general(
                hid[r * TOK:(r + 1) * TOK, :], wu[cols, :], NT, preferred_element_type=F32
            )
            low = low_lanes((160, 128))
            for q in (0, 1):
                even, lane = r * 8 + 4 * n + 2 * q, q * 384
                ci[even, 0:TOK, :] = term[:, lane:lane + 128].astype(BF)
                ci[even + 1, 0:TOK, :] = term[:, lane + 256:lane + 384].astype(BF)
                mid = term[:, lane + 128:lane + 256]
                top, bot = mid[0:160], swap_halves(mid[160:320])
                ci[even, TOK:BLK, :] = jnp.where(low, top, bot).astype(BF)
                ci[even + 1, TOK:BLK, :] = jnp.where(low, bot, top).astype(BF)

        loop(2, body)

    def down(lo, hi):
        def body(i):
            cols = pl.ds(pl.multiple_of((lo + i) * 256, 256), 256)
            dg[:, cols] = lax.dot_general(act[...], g[:, cols], TN, preferred_element_type=F32).astype(BF)

        loop(hi - lo, body)

    def upg(lo, hi):
        def body(i):
            cols = pl.ds(pl.multiple_of((lo + i) * 256, 256), 256)
            ug[cols, :] = lax.dot_general(xt[:, cols], hid[...], TN, preferred_element_type=F32).astype(BF)

        loop(hi - lo, body)

    def rs_push(block, index, to):
        pltpu.make_async_remote_copy(
            src_ref=ci.at[block], dst_ref=rs.at[index], send_sem=rs_send.at[index], recv_sem=rs_recv.at[index],
            device_id=to, device_id_type=MESH,
        ).start()

    def rs_add(block, *indices):
        total = ci[block].astype(F32)
        for index in indices:
            got(rs.at[index], rs_recv.at[index], dev_p(1))
            total = total + rs[index].astype(F32)
        return total

    def s_far(w, j):
        rs_push(slot(w, j, 2), (w * 4 + j) * 3, dev_s(1 if j in FWD else 3))

    def s_near(w, j):
        d = 3 if j in FWD else 1
        rs_push(slot(w, j, d), (w * 4 + j) * 3 + 2, dev_s(d))

    def s_mid(w, j):
        d, base = (1 if j in FWD else 3), (w * 4 + j) * 3
        block = slot(w, j, d)
        ci[block] = rs_add(block, base).astype(BF)
        rs_push(block, base + 1, dev_s(d))

    def s_end(w, j):
        base = (w * 4 + j) * 3
        block = slot(w, j, 0)
        ci[block] = rs_add(block, base + 1, base + 2).astype(BF)

    def p_open(w, j):
        d, base = (3 if w else 1), 24 + w * 3
        rs_push(slot(w, j, 0), base + (0 if j == 2 else 2), dev_p(d if j == 2 else 4 - d))

    def p_mid(w):
        d, base = (3 if w else 1), 24 + w * 3
        block = slot(w, d, 0)
        ci[block] = rs_add(block, base).astype(BF)
        rs_push(block, base + 1, dev_p(d))

    def p_end(w):
        base = 24 + w * 3
        block = slot(w, 0, 0)
        ci[block] = rs_add(block, base + 1, base + 2).astype(BF)
        if w:
            rs_push(block, 30, far_z)

    gathers = {"grad": grad, "tok": tok}
    steps = {
        "pre_send": preact_send, "pre_relay": preact_relay, "pre_get": preact_get, "activate": activate,
        "f1": f1, "f2": f2, "f3": f3, "f4": f4, "f5": f5, "f6": f6, "f7": f7,
        "unpack": lambda r: unpack(cx, xt, r), "down": down, "upg": upg,
    }
    scatter = {
        "far": s_far, "near": s_near, "mid": s_mid, "end": s_end,
        "p_open": p_open, "p_mid": p_mid, "p_end": p_end,
    }

    def run(name, *args):
        if name in gathers:
            gather = gathers[name]
            if args == (0, 0, 0):
                gather.start(0)
            elif args:
                gather.get(*args)
            else:
                gather.far()
        else:
            steps[name](*args)

    def by_core(core, work):
        if work:
            @pl.when(c == core)
            def _():
                for name, *args in work:
                    scatter[name](*args)

    packed = False
    for item in ORDER:
        if item[0] == "tok" and not packed:
            pack(tok_in, cx)
            packed = True
        if item[0] == "scatter":
            by_core(0, item[1])
            by_core(1, item[2])
        else:
            run(*item)
    total = rs_add(slot(0, 0, 0), 30)
    main, left, right = total[0:TOK], total[TOK:BLK, 0:64], total[TOK:BLK, 64:128]

    @pl.when(x % 2 == 0)
    def _():
        ig_out[0:128, :] = main.T.astype(BF)
        ig_out[128:192, :] = jnp.concatenate([left, right], axis=0).T.astype(BF)

    @pl.when(x % 2 == 1)
    def _():
        ig_out[64:192, :] = main.T.astype(BF)
        ig_out[0:64, :] = jnp.concatenate([right, left], axis=0).T.astype(BF)

    for copy in sent:
        copy.wait_send()
    for index in range(31):
        pltpu.make_async_remote_copy(
            src_ref=ci.at[0], dst_ref=rs.at[index], send_sem=rs_send.at[index], recv_sem=rs_recv.at[index],
            device_id=far_z, device_id_type=MESH,
        ).wait_send()


def per_device(inputs, out_grad, preact, up_weight, down_weight):
    vmem = pl.BlockSpec(memory_space=pltpu.VMEM)
    hbm = pl.BlockSpec(memory_space=pltpu.HBM)
    blocks = pltpu.VMEM((32, BLK, 128), BF)
    dma = pltpu.SemaphoreType.DMA
    tokens = 4 * TOK
    input_grad, up_grad, down_grad = pl.pallas_call(
        kernel,
        out_shape=(
            pltpu.VMEM((FEAT, TOK), BF),
            pltpu.VMEM((DI, HI), BF),
            pltpu.VMEM((HI, DI), BF),
        ),
        in_specs=[vmem, vmem, hbm, hbm, hbm],
        out_specs=(vmem, vmem, vmem),
        scratch_shapes=[
            blocks, blocks, blocks,
            pltpu.VMEM((31, BLK, 128), BF),
            pltpu.VMEM((tokens, DI), BF),
            pltpu.VMEM((tokens, DI), BF),
            pltpu.VMEM((HI, DI), BF),
            pltpu.VMEM((DI, HI), BF),
            pltpu.VMEM((4, TOK, HI), BF),
            pltpu.VMEM((4, 160, HI), BF),
            pltpu.VMEM((4, 80, HI), BF),
            pltpu.VMEM((4, 80, 384), BF),
            pltpu.VMEM((4, 160, HI), BF),
            pltpu.VMEM((4, 80, HI), BF),
            pltpu.VMEM((4, TOK, HI), BF),
            pltpu.VMEM((160, HI), BF),
            pltpu.VMEM((tokens, HI), BF),
            pltpu.VMEM((tokens, HI), BF),
            dma((2, 31)), dma((2, 2, 4, 4)),
            dma((31,)), dma((31,)),
            dma((6, 4)), dma((6, 4)),
            dma((7,)), dma((7,)),
            dma((8,)),
        ],
        compiler_params=pltpu.CompilerParams(
            collective_id=0, has_side_effects=True, vmem_limit_bytes=54 * 1024 * 1024
        ),
        name="ffn_backward",
    )(out_grad.T, inputs.T, preact, up_weight, down_weight)
    return input_grad.T, up_grad, down_grad


def solution(mesh):
    placed = (
        P("wa", ("ia", "ao")),
        P("wa", ("ia", "ao")),
        P("wa", "ao"),
        P("ia", ("ao", "wa")),
        P(("ao", "wa"), "ia"),
    )
    return jax.shard_map(
        per_device,
        mesh=mesh,
        in_specs=placed,
        out_specs=(P("wa", ("ia", "ao")), P("ia", ("ao", "wa")), P(("ao", "wa"), "ia")),
        check_vma=False,
    )
```

```python
import jax
import jax.numpy as jnp
from jax import lax
from jax.experimental import pallas as pl
from jax.experimental.pallas import tpu as pltpu
from jax.sharding import PartitionSpec as P

MESH = pl.DeviceIdType.MESH
BF = jnp.bfloat16
F32 = jnp.float32
TOK = 320
FEAT = 192
BLK = 480
DI = 1536
HI = 768
NT = (((1,), (1,)), ((), ()))
TN = (((0,), (0,)), ((), ()))
FWD = (0, 3)

ORDER = (
    ("grad", 0, 0, 0), ("grad",), ("grad", 0, 3, 0), ("grad", 0, 1, 0), ("grad", 1, 0, 0), ("tok",),
    ("grad", 0, 0, 3), ("grad", 0, 2, 0), ("grad", 1, 0, 3), ("grad", 1, 1, 0), ("grad", 1, 3, 0),
    ("grad", 0, 0, 2), ("grad", 0, 1, 1), ("activate", 0), ("grad", 0, 3, 1), ("grad", 0, 0, 1),
    ("grad", 1, 0, 1), ("grad", 0, 3, 3), ("grad", 1, 0, 2), ("grad", 1, 2, 0), ("grad", 1, 1, 1), ("f1", 0),
    ("grad", 1, 3, 3), ("grad", 0, 1, 2), ("grad", 0, 2, 1), ("grad", 1, 2, 1), ("pre_send",), ("grad", 1, 1, 3),
    ("f2", 0), ("grad", 0, 1, 3), ("grad", 1, 1, 2), ("grad", 1, 3, 1), ("f1", 1), ("grad", 0, 2, 2),
    ("grad", 0, 2, 3), ("grad", 0, 3, 2), ("tok", 1, 0, 0), ("grad", 1, 3, 2), ("grad", 1, 2, 3), ("f3", 0),
    ("f2", 1), ("grad", 1, 2, 2), ("f1", 2), ("pre_relay",), ("f4", 0), ("tok", 0, 0, 0), ("f2", 2), ("f3", 1),
    ("pre_get", 1), ("tok", 1, 1, 0), ("f5", 0), ("f1", 3), ("f3", 2), ("tok", 0, 3, 0), ("f4", 1),
    ("tok", 0, 1, 0), ("pre_get", 2), ("tok", 0, 0, 1), ("tok", 0, 0, 3), ("f2", 3), ("activate", 1), ("f6", 0),
    ("f4", 2), ("tok", 1, 2, 0), ("tok", 0, 2, 0), ("f5", 1), ("tok", 0, 3, 3), ("tok", 0, 1, 3),
    ("tok", 1, 3, 0), ("tok", 0, 1, 1), ("f3", 3), ("f7", 0), ("tok", 1, 0, 3), ("f5", 2), ("f6", 1),
    ("pre_get", 3), ("tok", 0, 2, 1), ("tok", 1, 2, 1),
    ("scatter",
     (),
     (("near", 1, 0), ("far", 0, 0),)),
    ("f4", 3), ("tok", 0, 2, 3), ("tok", 1, 3, 3), ("f7", 1), ("f6", 2),
    ("scatter",
     (("near", 1, 2),),
     (("far", 1, 0), ("far", 0, 1), ("far", 1, 1),)),
    ("tok", 1, 2, 3),
    ("scatter",
     (),
     (("near", 0, 1),)),
    ("f5", 3), ("tok", 1, 1, 1), ("tok", 0, 3, 2),
    ("scatter",
     (("near", 0, 2),),
     ()),
    ("tok", 1, 0, 2), ("activate", 3), ("f7", 2),
    ("scatter",
     (("far", 1, 3), ("far", 1, 1),),
     (("mid", 1, 0),)),
    ("f6", 3),
    ("scatter",
     (),
     (("near", 1, 1),)),
    ("activate", 2),
    ("scatter",
     (("far", 1, 2),),
     ()),
    ("tok", 0, 3, 1),
    ("scatter",
     (("far", 1, 0), ("far", 0, 0), ("far", 0, 1), ("far", 0, 3), ("near", 1, 1),),
     (("far", 1, 2),)),
    ("tok", 1, 3, 1), ("tok", 0, 0, 2),
    ("scatter",
     (("far", 0, 2),),
     (("mid", 1, 1), ("mid", 0, 0),)),
    ("tok", 1, 1, 2), ("f7", 3),
    ("scatter",
     (("mid", 1, 2),),
     (("far", 1, 3), ("near", 1, 3), ("near", 1, 2), ("mid", 1, 2),)),
    ("down", 0, 1),
    ("scatter",
     (("mid", 1, 1), ("near", 0, 3),),
     (("far", 0, 3), ("end", 1, 0),)),
    ("down", 1, 2),
    ("scatter",
     (("mid", 1, 3), ("mid", 0, 0),),
     (("far", 0, 2), ("end", 1, 1),)),
    ("tok", 1, 1, 3),
    ("scatter",
     (("near", 1, 3),),
     ()),
    ("down", 2, 3),
    ("scatter",
     (("end", 1, 2), ("p_open", 1, 2), ("mid", 0, 2),),
     (("mid", 1, 3),)),
    ("down", 3, 4),
    ("scatter",
     (),
     (("end", 1, 2),)),
    ("tok", 1, 3, 2),
    ("scatter",
     (("mid", 1, 0), ("end", 1, 1), ("p_open", 1, 1), ("near", 1, 0),),
     (("p_open", 1, 2),)),
    ("down", 4, 5), ("tok", 1, 0, 1),
    ("scatter",
     (("mid", 0, 3), ("end", 1, 3), ("p_mid", 1), ("near", 0, 0),),
     (("near", 0, 2), ("mid", 0, 2),)),
    ("unpack", 0),
    ("scatter",
     (),
     (("p_open", 1, 1),)),
    ("tok", 0, 1, 2),
    ("scatter",
     (),
     (("mid", 0, 3),)),
    ("unpack", 3),
    ("scatter",
     (),
     (("end", 1, 3), ("mid", 0, 1), ("p_mid", 1),)),
    ("tok", 1, 2, 2), ("tok", 0, 2, 2),
    ("scatter",
     (("end", 0, 2),),
     ()),
    ("unpack", 2),
    ("scatter",
     (("near", 0, 1), ("mid", 0, 1),),
     (("near", 0, 3),)),
    ("unpack", 1),
    ("scatter",
     (("p_open", 0, 2), ("end", 1, 0), ("p_end", 1),),
     (("near", 0, 0), ("end", 0, 2), ("p_open", 0, 2),)),
    ("upg", 0, 2),
    ("scatter",
     (),
     (("p_end", 1),)),
    ("upg", 2, 3),
    ("scatter",
     (("end", 0, 3), ("p_open", 0, 3), ("end", 0, 1), ("p_mid", 0), ("end", 0, 0),),
     (("end", 0, 1), ("p_mid", 0), ("end", 0, 0), ("end", 0, 3), ("p_open", 0, 3),)),
    ("down", 5, 6), ("upg", 3, 6),
    ("scatter",
     (("p_end", 0),),
     (("p_end", 0),)),
)


def gelu(u):
    square = u * u
    t = jnp.tanh(0.7978845608 * (u + 0.044715 * u * square))
    return 0.5 * u * (1.0 + t)


def slope(u):
    square = u * u
    t = jnp.tanh(0.7978845608 * (u + 0.044715 * u * square))
    return 0.5 * (1.0 + t) + 0.5 * u * (1.0 - t * t) * 0.7978845608 * (1.0 + 0.134145 * square)


def swap_halves(v):
    return pltpu.roll(v, 64, 1)


def low_lanes(shape):
    return lax.broadcasted_iota(jnp.int32, shape, 1) < 64


def loop(n, body):
    def step(i, carry):
        body(i)
        return carry

    lax.fori_loop(0, n, step, 0)


def kernel(
    grad_in, tok_in, preact, up_w, down_w,
    ig_out, ug, dg,
    cg, cx, ci, rs, g, xt, wd, wu, par, rc, r1, r2, s1, s2, pre, stage, act, hid,
    ag_send, ag_recv, rs_send, rs_recv, f_send, f_recv, p_send, p_recv, l_sem,
):
    ia, y, ao = lax.axis_index("ia"), lax.axis_index("wa"), lax.axis_index("ao")
    zl, c = ia // 2, ia % 2
    zh, x = ao // 4, ao % 4
    b0, b1 = zl % 2, zl // 2

    def dev(dx=0, dy=0, flip_zh=False, to_zl=None, flip_c=False):
        x_, y_ = (x + dx) % 4, (y + dy) % 4
        zh_ = 1 - zh if flip_zh else zh
        zl_ = zl if to_zl is None else to_zl
        c_ = 1 - c if flip_c else c
        return {"ia": zl_ * 2 + c_, "wa": y_, "ao": zh_ * 4 + x_}

    def dev_p(d):
        return dev(dx=d * (1 - c), dy=d * c)

    def dev_s(d):
        return dev(dx=d * c, dy=d * (1 - c))

    sibling = dev(flip_c=True)
    far_z = dev(flip_zh=True)
    zl1 = dev(to_zl=zl + 1 - 2 * b0)
    zl2 = dev(to_zl=zl + 2 - 4 * b1)

    sent = []

    def push(src, dst, ssem, rsem, to):
        copy = pltpu.make_async_remote_copy(
            src_ref=src, dst_ref=dst, send_sem=ssem, recv_sem=rsem, device_id=to, device_id_type=MESH
        )
        copy.start()
        sent.append(copy)

    def got(dst, rsem, frm):
        pltpu.make_async_remote_copy(
            src_ref=dst, dst_ref=dst, send_sem=l_sem.at[7], recv_sem=rsem, device_id=frm, device_id_type=MESH
        ).wait_recv()

    copies = [
        pltpu.make_async_copy(down_w, wd, l_sem.at[0]),
        pltpu.make_async_copy(up_w, wu, l_sem.at[1]),
        pltpu.make_async_copy(
            preact.at[:, pl.ds(pl.multiple_of(y * HI, 128), HI)], pre.at[0], l_sem.at[2]
        ),
    ]
    for copy in copies:
        copy.start()
    waiting = {0, 1, 2}

    def loaded(n):
        if n in waiting:
            waiting.remove(n)
            copies[n].wait()

    def slot(w, j, k, jr=None, kr=None):
        jr, kr = (j if jr is None else jr), (k if kr is None else kr)
        dx, dy = j + (k - j) * c, kr + (jr - kr) * c
        zh_ = 1 - zh if w else zh
        return dy * 8 + zh_ * 4 + (x + dx) % 4

    def pack(src, dst):
        own = slot(0, 0, 0)

        def place(main, mini, first, second):
            dst[own, 0:TOK, :] = src[main:main + 128, :].astype(F32).T.astype(BF)
            m = src[mini:mini + 64, :].astype(F32).T
            halves = (m[0:160], m[160:320])
            dst[own, TOK:BLK, :] = jnp.concatenate([halves[first], halves[second]], axis=1).astype(BF)

        @pl.when(x % 2 == 0)
        def _():
            place(0, 128, 0, 1)

        @pl.when(x % 2 == 1)
        def _():
            place(64, 0, 1, 0)

    def unpack(src, dst, r):
        def body(n):
            e = src.at[r * 8 + 2 * n]
            o = src.at[r * 8 + 2 * n + 1]
            rows = pl.ds(r * TOK, TOK)
            base = n * 384
            dst[rows, pl.ds(pl.multiple_of(base, 128), 128)] = e[0:TOK, :]
            dst[rows, pl.ds(pl.multiple_of(base + 256, 128), 128)] = o[0:TOK, :]
            p, q = e[TOK:BLK, :].astype(F32), o[TOK:BLK, :].astype(F32)
            low = low_lanes((160, 128))
            mid = pl.ds(pl.multiple_of(base + 128, 128), 128)
            dst[pl.ds(r * TOK, 160), mid] = jnp.where(low, p, q).astype(BF)
            dst[pl.ds(r * TOK + 160, 160), mid] = swap_halves(jnp.where(low, q, p)).astype(BF)

        loop(4, body)

    pack(grad_in, cg)

    barrier = pltpu.get_barrier_semaphore()
    partners = [dev_p(1), dev_p(3), dev_s(1), dev_s(3), dev(dy=2), sibling, far_z, zl1, zl2]
    for partner in partners[0:4] + partners[5:]:
        pl.semaphore_signal(barrier, inc=1, device_id=partner, device_id_type=MESH)
    pl.semaphore_wait(barrier, 8)

    class Gather:
        def __init__(self, index, buf):
            self.index, self.buf, self.n, self.have = index, buf, 0, {(0, 0, 0)}

        def _push(self, w, j, k, jr, kr, to, wr=None):
            push(
                self.buf.at[slot(w, j, k)],
                self.buf.at[slot(w, j, k, jr, kr)],
                ag_send.at[self.index, self.n],
                ag_recv.at[self.index, w if wr is None else wr, jr, kr],
                to,
            )
            self.n += 1

        def p(self, w, j, d):
            self._push(w, j, 0, (j - d) % 4, 0, dev_p(d))

        def s(self, w, j, k, d):
            self._push(w, j, k, j, (k - d) % 4, dev_s(d))

        def far(self):
            self._push(0, 0, 0, 0, 0, far_z, wr=1)

        def get(self, w, j, k):
            if (w, j, k) in self.have:
                return
            self.have.add((w, j, k))
            got(self.buf.at[slot(w, j, k)], ag_recv.at[self.index, w, j, k], dev_p(1))
            if k == 0:
                if j == 0:
                    self.start(w)
                    return
                if w == 0 and j == 3:
                    self.p(w, j, 1)
                if w == 1 and j == 1:
                    self.p(w, j, 3)
                self.s(w, j, k, 1)
                self.s(w, j, k, 3)
            elif k == 3 and j in FWD:
                self.s(w, j, k, 1)
            elif k == 1 and j not in FWD:
                self.s(w, j, k, 3)

        def start(self, w):
            for d in (1, 3):
                self.p(w, 0, d)
                self.s(w, 0, 0, d)

        def tokens(self, r):
            for w in (0, 1):
                for i in (0, 1, 3, 2):
                    self.get(w, i, r)
                for i in (0, 1, 3, 2):
                    self.get(w, r, i)

    grad, tok = Gather(0, cg), Gather(1, cx)

    half = pl.ds(pl.multiple_of(c * 160, 16), 160)
    other = pl.ds(pl.multiple_of((1 - c) * 160, 16), 160)
    up = 1 + 2 * c

    def preact_send():
        def cols(d):
            return pl.ds(pl.multiple_of(((y + d) % 4) * HI, 128), HI)

        push(preact.at[half, cols(2)], stage, p_send.at[0], p_recv.at[0], dev(dy=up))
        for d in (1, 3):
            push(preact.at[half, cols(d)], pre.at[4 - d, half], p_send.at[d], p_recv.at[4 - d], dev(dy=d))

    def preact_relay():
        got(stage, p_recv.at[0], dev(dy=1))
        push(stage, pre.at[2, half], p_send.at[2], p_recv.at[2], dev(dy=up))

    def preact_get(r):
        got(pre.at[r, half], p_recv.at[r], dev(dy=1))
        push(pre.at[r, half], pre.at[r, half], p_send.at[3 + r], p_recv.at[3 + r], sibling)

    def activate(r):
        if r > 0:
            got(pre.at[r, other], p_recv.at[3 + r], sibling)
        else:
            loaded(2)

        def body(i):
            rows = pl.multiple_of(i * 32, 32)
            u = pre[r, pl.ds(rows, 32), :].astype(F32)
            act[pl.ds(r * TOK + rows, 32), :] = gelu(u).astype(BF)

        loop(10, body)

    rows80 = pl.ds(pl.multiple_of(c * 160 + b0 * 80, 16), 80)
    keep80, give80 = pl.ds(pl.multiple_of(b0 * 80, 16), 80), pl.ds(pl.multiple_of((1 - b0) * 80, 16), 80)
    peer80 = pl.ds(pl.multiple_of(c * 160 + (1 - b0) * 80, 16), 80)
    keep384 = pl.ds(pl.multiple_of(b1 * 384, 128), 384)
    give384 = pl.ds(pl.multiple_of((1 - b1) * 384, 128), 384)

    def f1(r):
        grad.tokens(r)
        unpack(cg, g, r)
        loaded(0)

        def body(n):
            cols = pl.ds(pl.multiple_of(n * 256, 256), 256)
            par[r, :, cols] = lax.dot_general(
                g[r * TOK:(r + 1) * TOK, :], wd[cols, :], NT, preferred_element_type=F32
            ).astype(BF)

        loop(3, body)
        push(par.at[r, other], rc.at[r], f_send.at[0, r], f_recv.at[0, r], sibling)

    def f2(r):
        got(rc.at[r], f_recv.at[0, r], sibling)
        s1[r] = (par[r, half, :].astype(F32) + rc[r].astype(F32)).astype(BF)
        push(s1.at[r, give80], r1.at[r], f_send.at[1, r], f_recv.at[1, r], zl1)

    def f3(r):
        got(r1.at[r], f_recv.at[1, r], zl1)
        s2[r] = (s1[r, keep80, :].astype(F32) + r1[r].astype(F32)).astype(BF)
        push(s2.at[r, :, give384], r2.at[r], f_send.at[2, r], f_recv.at[2, r], zl2)

    def hrows(r, ds):
        return pl.ds(pl.multiple_of(r * TOK + ds.start, 16), ds.size)

    def f4(r):
        if r == 0:
            loaded(2)
        got(r2.at[r], f_recv.at[2, r], zl2)
        total = s2[r, :, keep384].astype(F32) + r2[r].astype(F32)
        u = pre[r, rows80, keep384].astype(F32)
        hid[hrows(r, rows80), keep384] = (total * slope(u)).astype(BF)
        piece = hid.at[hrows(r, rows80), keep384]
        push(piece, piece, f_send.at[3, r], f_recv.at[3, r], zl2)

    def f5(r):
        got(hid.at[hrows(r, rows80), give384], f_recv.at[3, r], zl2)
        piece = hid.at[hrows(r, rows80), :]
        push(piece, piece, f_send.at[4, r], f_recv.at[4, r], zl1)

    def f6(r):
        got(hid.at[hrows(r, peer80), :], f_recv.at[4, r], zl1)
        piece = hid.at[hrows(r, half), :]
        push(piece, piece, f_send.at[5, r], f_recv.at[5, r], sibling)

    def f7(r):
        got(hid.at[hrows(r, other), :], f_recv.at[5, r], sibling)
        loaded(1)

        def body(n):
            cols = pl.ds(pl.multiple_of(n * 768, 256), 768)
            term = lax.dot_general(
                hid[r * TOK:(r + 1) * TOK, :], wu[cols, :], NT, preferred_element_type=F32
            )
            low = low_lanes((160, 128))
            for q in (0, 1):
                even, lane = r * 8 + 4 * n + 2 * q, q * 384
                ci[even, 0:TOK, :] = term[:, lane:lane + 128].astype(BF)
                ci[even + 1, 0:TOK, :] = term[:, lane + 256:lane + 384].astype(BF)
                mid = term[:, lane + 128:lane + 256]
                top, bot = mid[0:160], swap_halves(mid[160:320])
                ci[even, TOK:BLK, :] = jnp.where(low, top, bot).astype(BF)
                ci[even + 1, TOK:BLK, :] = jnp.where(low, bot, top).astype(BF)

        loop(2, body)

    def down(lo, hi):
        def body(i):
            cols = pl.ds(pl.multiple_of((lo + i) * 256, 256), 256)
            dg[:, cols] = lax.dot_general(act[...], g[:, cols], TN, preferred_element_type=F32).astype(BF)

        loop(hi - lo, body)

    def upg(lo, hi):
        def body(i):
            cols = pl.ds(pl.multiple_of((lo + i) * 256, 256), 256)
            ug[cols, :] = lax.dot_general(xt[:, cols], hid[...], TN, preferred_element_type=F32).astype(BF)

        loop(hi - lo, body)

    def rs_push(block, index, to):
        pltpu.make_async_remote_copy(
            src_ref=ci.at[block], dst_ref=rs.at[index], send_sem=rs_send.at[index], recv_sem=rs_recv.at[index],
            device_id=to, device_id_type=MESH,
        ).start()

    def rs_add(block, *indices):
        total = ci[block].astype(F32)
        for index in indices:
            got(rs.at[index], rs_recv.at[index], dev_p(1))
            total = total + rs[index].astype(F32)
        return total

    def s_far(w, j):
        rs_push(slot(w, j, 2), (w * 4 + j) * 3, dev_s(1 if j in FWD else 3))

    def s_near(w, j):
        d = 3 if j in FWD else 1
        rs_push(slot(w, j, d), (w * 4 + j) * 3 + 2, dev_s(d))

    def s_mid(w, j):
        d, base = (1 if j in FWD else 3), (w * 4 + j) * 3
        block = slot(w, j, d)
        ci[block] = rs_add(block, base).astype(BF)
        rs_push(block, base + 1, dev_s(d))

    def s_end(w, j):
        base = (w * 4 + j) * 3
        block = slot(w, j, 0)
        ci[block] = rs_add(block, base + 1, base + 2).astype(BF)

    def p_open(w, j):
        d, base = (3 if w else 1), 24 + w * 3
        rs_push(slot(w, j, 0), base + (0 if j == 2 else 2), dev_p(d if j == 2 else 4 - d))

    def p_mid(w):
        d, base = (3 if w else 1), 24 + w * 3
        block = slot(w, d, 0)
        ci[block] = rs_add(block, base).astype(BF)
        rs_push(block, base + 1, dev_p(d))

    def p_end(w):
        base = 24 + w * 3
        block = slot(w, 0, 0)
        ci[block] = rs_add(block, base + 1, base + 2).astype(BF)
        if w:
            rs_push(block, 30, far_z)

    gathers = {"grad": grad, "tok": tok}
    steps = {
        "pre_send": preact_send, "pre_relay": preact_relay, "pre_get": preact_get, "activate": activate,
        "f1": f1, "f2": f2, "f3": f3, "f4": f4, "f5": f5, "f6": f6, "f7": f7,
        "unpack": lambda r: unpack(cx, xt, r), "down": down, "upg": upg,
    }
    scatter = {
        "far": s_far, "near": s_near, "mid": s_mid, "end": s_end,
        "p_open": p_open, "p_mid": p_mid, "p_end": p_end,
    }

    def run(name, *args):
        if name in gathers:
            gather = gathers[name]
            if args == (0, 0, 0):
                gather.start(0)
            elif args:
                gather.get(*args)
            else:
                gather.far()
        else:
            steps[name](*args)

    def by_core(core, work):
        if work:
            @pl.when(c == core)
            def _():
                for name, *args in work:
                    scatter[name](*args)

    packed = False
    for item in ORDER:
        if item[0] == "tok" and not packed:
            pack(tok_in, cx)
            packed = True
        if item[0] == "scatter":
            by_core(0, item[1])
            by_core(1, item[2])
        else:
            run(*item)
    total = rs_add(slot(0, 0, 0), 30)
    main, left, right = total[0:TOK], total[TOK:BLK, 0:64], total[TOK:BLK, 64:128]

    @pl.when(x % 2 == 0)
    def _():
        ig_out[0:128, :] = main.T.astype(BF)
        ig_out[128:192, :] = jnp.concatenate([left, right], axis=0).T.astype(BF)

    @pl.when(x % 2 == 1)
    def _():
        ig_out[64:192, :] = main.T.astype(BF)
        ig_out[0:64, :] = jnp.concatenate([right, left], axis=0).T.astype(BF)

    for copy in sent:
        copy.wait_send()
    for index in range(31):
        pltpu.make_async_remote_copy(
            src_ref=ci.at[0], dst_ref=rs.at[index], send_sem=rs_send.at[index], recv_sem=rs_recv.at[index],
            device_id=far_z, device_id_type=MESH,
        ).wait_send()


def per_device(inputs, out_grad, preact, up_weight, down_weight):
    vmem = pl.BlockSpec(memory_space=pltpu.VMEM)
    hbm = pl.BlockSpec(memory_space=pltpu.HBM)
    blocks = pltpu.VMEM((32, BLK, 128), BF)
    dma = pltpu.SemaphoreType.DMA
    tokens = 4 * TOK
    input_grad, up_grad, down_grad = pl.pallas_call(
        kernel,
        out_shape=(
            pltpu.VMEM((FEAT, TOK), BF),
            pltpu.VMEM((DI, HI), BF),
            pltpu.VMEM((HI, DI), BF),
        ),
        in_specs=[vmem, vmem, hbm, hbm, hbm],
        out_specs=(vmem, vmem, vmem),
        scratch_shapes=[
            blocks, blocks, blocks,
            pltpu.VMEM((31, BLK, 128), BF),
            pltpu.VMEM((tokens, DI), BF),
            pltpu.VMEM((tokens, DI), BF),
            pltpu.VMEM((HI, DI), BF),
            pltpu.VMEM((DI, HI), BF),
            pltpu.VMEM((4, TOK, HI), BF),
            pltpu.VMEM((4, 160, HI), BF),
            pltpu.VMEM((4, 80, HI), BF),
            pltpu.VMEM((4, 80, 384), BF),
            pltpu.VMEM((4, 160, HI), BF),
            pltpu.VMEM((4, 80, HI), BF),
            pltpu.VMEM((4, TOK, HI), BF),
            pltpu.VMEM((160, HI), BF),
            pltpu.VMEM((tokens, HI), BF),
            pltpu.VMEM((tokens, HI), BF),
            dma((2, 31)), dma((2, 2, 4, 4)),
            dma((31,)), dma((31,)),
            dma((6, 4)), dma((6, 4)),
            dma((7,)), dma((7,)),
            dma((8,)),
        ],
        compiler_params=pltpu.CompilerParams(
            collective_id=0, has_side_effects=True, vmem_limit_bytes=54 * 1024 * 1024
        ),
        name="ffn_backward",
    )(out_grad.T, inputs.T, preact, up_weight, down_weight)
    return input_grad.T, up_grad, down_grad


def solution(mesh):
    placed = (
        P("wa", ("ia", "ao")),
        P("wa", ("ia", "ao")),
        P("wa", "ao"),
        P("ia", ("ao", "wa")),
        P(("ao", "wa"), "ia"),
    )
    return jax.shard_map(
        per_device,
        mesh=mesh,
        in_specs=placed,
        out_specs=(P("wa", ("ia", "ao")), P("ia", ("ao", "wa")), P(("ao", "wa"), "ia")),
        check_vma=False,
    )
```
